256 devices in a mesh: phase: 2 (over x_hi), bank: 16 (over x_lo, y, core), blk: 8 (over z).
Axes of the slice: x: 4 (x_hi: 2, x_lo: 2; x = x_hi * 2 + x_lo), y: 4, z: 8, core: 2. Of those that a mesh axis runs over, the one named last changes fastest.
Arguments:
- query_clips: bfloat16 [16, 1024, 128], P('blk', 'bank'), may hold values from -6 to 6
- conv_weight: bfloat16 [4, 3, 1024, 32], P('phase', None, 'bank'), may hold values from -0.625 to 0.625
- mix_weight: bfloat16 [4, 1024, 1024], P('phase', 'bank'), may hold values from -0.1875 to 0.1875
- proj_weight: bfloat16 [512, 1024], P(None, 'bank'), may hold values from -0.25 to 0.25
- taps: float32 [7], replicated, may hold values from 0.25 to 1
- reference_frames: bfloat16 [524288, 512], P(('phase', 'bank', 'blk')), may hold values from -6 to 6
- slice_lengths: int32 [256, 16], P(('phase', 'bank', 'blk')), may hold values from 1 to 256, 2048 in all within a row
Outputs:
- tile_maxima: float32 [16, 4096], P(None, ('phase', 'bank', 'blk'))
The draws below stay inside these ranges and needn't reach their ends.
Inputs may be any that keep to these rules, and one draw needn't show every extreme that they name: `slice_lengths`: each row sums to 2048, and the largest entry of every row is 256.
All inputs are finite; a program needn't handle non-finite values.
Results may differ from the reference program's by a relative error of at most 0.004.
Values may be sent and summed in bfloat16 or wider, within the bound.
A program may use at most 64 MiB of HBM per device.

```python
import math
import jax
import jax.numpy as jnp
import numpy as np
from jax import lax

C = 1024
GROUPS = 32
E = 512
LAYERS = 4
QL = 128
F_DEV = 2048
SLICES = 16
TILE = 128
TAPS = 7
NCLIP = 16
REF = 524288
TILES = 4096
SLICE_MOST = 256
DEVICES = 256


def raised(array, rng, source, target, parts, factor):
    owner, partner = [(jnp.arange(array.shape[axis_at]) // (array.shape[axis_at] // parts)).reshape([-1 if axis == axis_at else 1 for axis in range(array.ndim)]) for axis_at in (source, target)]
    chosen = jax.random.permutation(rng, parts)[partner]
    strong = (owner == chosen) | (owner == (partner + parts // 2) % parts)
    return jnp.where(strong, factor * array, array)


def block_levels(own_key, dims, shards, smallest, high):
    level, own = 1.0, jax.random.fold_in(own_key, 6)
    for axis_at, blocks in shards:
        heights = jnp.exp(jax.random.uniform(jax.random.fold_in(own, axis_at), (blocks,), jnp.float32, smallest / len(shards), high / len(shards)))
        level = level * jnp.repeat(heights, dims[axis_at] // blocks).reshape([-1 if axis == axis_at else 1 for axis in range(len(dims))])
    return level


def profile(count, total, limit, slope):
    weights = [(1 << 20) // math.isqrt(standing ** slope) + 1 for standing in range(2, count + 1)]
    spare, holding = total - limit - (count - 1), [1] * (count - 1)
    while spare > 0:
        free = [i for i in range(count - 1) if holding[i] < limit]
        pool, remaining = sum([weights[i] for i in free]), spare
        for i in free:
            more = min(limit - holding[i], max(1, remaining * weights[i] // pool), spare)
            holding[i] = holding[i] + more
            spare = spare - more
    return np.array([limit] + holding)


def uneven(stream_key, amount, total, reach, skew):
    if amount == 2:
        one = jax.random.randint(stream_key, (), max(1, total - reach), min(reach, total - 1) + 1)
        return jnp.stack([one, total - one])
    sizes = jnp.asarray(profile(amount, total, reach, skew), jnp.int32)
    twos = (amount - 1) // 2
    donor, receiver = sizes[1:1 + 2 * twos:2], sizes[2:2 + 2 * twos:2]
    margin = jnp.minimum(donor - 1, reach - receiver)
    shifted = jax.random.randint(jax.random.fold_in(stream_key, 1), (twos,), 0, 1 << 20) % (margin + 1)
    sizes = sizes.at[1:1 + 2 * twos:2].set(donor - shifted).at[2:2 + 2 * twos:2].set(receiver + shifted)
    return sizes[jax.random.permutation(jax.random.fold_in(stream_key, 2), amount)]


def bell_draw(stream_key, extent, width, most, pieces=(), held_as=jnp.bfloat16):
    drawn = jax.random.normal(stream_key, extent, jnp.float32) * width
    if len(pieces) > 0:
        drawn = block_levels(stream_key, extent, pieces, -0.22, 0.18) * drawn
    return jnp.clip(drawn, min=-most, max=most).astype(held_as)


def bell_draw_with(key, extent, deviation, most, cuts, heavy, held_as=jnp.bfloat16):
    result = deviation * jax.random.normal(key, extent, jnp.float32)
    if cuts:
        result = result * block_levels(key, extent, cuts, -0.22, 0.18)
    return jnp.clip(raised(result, jax.random.fold_in(key, 3), *heavy), -most, most).astype(held_as)


def setup_inputs(seed: int = 0) -> dict:
    streams_of = jax.random.split(jax.random.key(seed), 8)
    query_clips = bell_draw(streams_of[0], (NCLIP, C, QL), 1.0, 6.0, ((0, 8), (1, 16)))
    conv_weight = bell_draw(streams_of[1], (LAYERS, 3, C, C // GROUPS), (3 * (C // GROUPS)) ** -0.5, 0.625, ((0, 2), (2, 16)))
    mix_weight = bell_draw(streams_of[2], (LAYERS, C, C), C ** -0.5, 0.1875, ((0, 2), (1, 16)))
    proj_weight = bell_draw_with(streams_of[3], (E, C), C ** -0.5, 0.25, ((1, 16),), (1, 0, 16, 2.0))
    taps = jnp.clip(jax.random.uniform(streams_of[4], (TAPS,), jnp.float32, 0.25, 1.0), 0.25, 1.0)
    reference_frames = bell_draw(streams_of[5], (REF, E), 1.0, 6.0, ((0, 256),))
    slice_lengths = jax.vmap(lambda own: uneven(own, SLICES, F_DEV, SLICE_MOST, 2))(jax.random.split(streams_of[6], DEVICES)).reshape((DEVICES, SLICES)).astype(jnp.int32)
    return {"query_clips": query_clips, "conv_weight": conv_weight, "mix_weight": mix_weight, "proj_weight": proj_weight, "taps": taps, "reference_frames": reference_frames, "slice_lengths": slice_lengths}


def encode_layer(hidden_state, conv_layer, mix_layer, dilation):
    group_width = C // GROUPS
    clip_count = hidden_state.shape[0]
    padded = jnp.pad(hidden_state, ((0, 0), (0, 0), (dilation, dilation)))
    kernels = conv_layer.astype(jnp.float32).reshape(3, GROUPS, group_width, group_width)
    summed = jnp.zeros((clip_count, GROUPS, group_width, QL), jnp.float32)
    for tap_index in range(3):
        window = padded[:, :, tap_index * dilation:tap_index * dilation + QL]
        window = window.astype(jnp.float32).reshape(clip_count, GROUPS, group_width, QL)
        summed = summed + jnp.einsum('ngit,goi->ngot', window, kernels[tap_index])
    activated = jax.nn.gelu(summed, approximate=True).astype(jnp.bfloat16).reshape(clip_count, C, QL)
    widened = activated.astype(jnp.float32)
    factor = lax.rsqrt(lax.optimization_barrier(jnp.sum(widened * widened, axis=1)) / C + 1e-06)
    mixed_sum = jnp.einsum('oc,nct->not', mix_layer.astype(jnp.float32), widened) * factor[:, None, :]
    return (hidden_state.astype(jnp.float32) + mixed_sum).astype(jnp.bfloat16)

def filtered_maxima(descriptors, frames, lengths, taps):
    frame_count = frames.shape[0]
    clip_count = descriptors.shape[0]
    scores = jnp.einsum('net,re->ntr', descriptors.astype(jnp.float32), frames.astype(jnp.float32)) * E ** (-0.5)
    slice_ends = jnp.cumsum(lengths).astype(jnp.int32)
    position = jnp.arange(frame_count, dtype=jnp.int32)
    segment = lax.optimization_barrier(jnp.sum((position[:, None] >= slice_ends[None, :]).astype(jnp.int32), axis=1)).astype(jnp.int32)
    segment_pad = jnp.pad(segment, (3, 3), constant_values=-1)
    padded = jnp.pad(scores, ((0, 0), (3, 3), (3, 3)))
    filtered = jnp.zeros_like(scores)
    for shift_index in range(TAPS):
        same_slice = segment_pad[shift_index:shift_index + frame_count] == segment
        moved = padded[:, shift_index:shift_index + QL, shift_index:shift_index + frame_count]
        filtered = filtered + taps[shift_index] * jnp.where(same_slice[None, None, :], moved, 0.0)
    return lax.optimization_barrier(jnp.max(filtered.reshape(clip_count, QL, frame_count // TILE, TILE), axis=(1, 3)))

def reference(query_clips, conv_weight, mix_weight, proj_weight, taps, reference_frames, slice_lengths):
    hidden_state = query_clips
    for layer_index in range(LAYERS):
        hidden_state = encode_layer(hidden_state, conv_weight[layer_index], mix_weight[layer_index], 2 ** layer_index)
    projected = jnp.einsum('ec,nct->net', proj_weight.astype(jnp.float32), hidden_state.astype(jnp.float32))
    norm_sums = lax.optimization_barrier(jnp.sum(projected * projected, axis=1)) / E
    descriptors = (projected * lax.rsqrt(norm_sums + 1e-06)[:, None, :]).astype(jnp.bfloat16)
    blocks_all = reference_frames.reshape(DEVICES, F_DEV, E)

    def one_block(operands):
        frames, lengths = operands
        return filtered_maxima(descriptors, frames, lengths, taps)
    maxima_all = lax.map(one_block, (blocks_all, slice_lengths))
    return jnp.transpose(maxima_all, (1, 0, 2)).reshape(NCLIP, TILES)
```

```python
import functools

import jax
import jax.numpy as jnp
from jax import lax
from jax.experimental import pallas as pl
from jax.experimental.pallas import tpu as pltpu
from jax.sharding import PartitionSpec as P

BF = jnp.bfloat16
F32 = jnp.float32
TAPS = 7
SUB = 8
PAD = 4
STEPS = 4
GROUP = 8


def kernel(
    G, Z, q_ref, cw_ref, mw_ref, pw_ref, taps_ref, rf_ref, sl_ref, out_ref,
    wmix, wconv, wown, wsib, wproj, hin, hout, U, D, rbuf, r32, rperm, wtab, s0, s1, acc,
    loc, sib_s, sib_r, gat_s, gat_r, ph_s, ph_r, ring_s, ring_r,
):
    half_ch = q_ref.shape[1]
    ch = 2 * half_ch
    T = q_ref.shape[2]
    C = mw_ref.shape[2]
    E = pw_ref.shape[0]
    F = rf_ref.shape[0]
    slices = sl_ref.shape[1]
    gw = cw_ref.shape[3]
    LO = F // SUB
    rows_all = (LO + 2 * PAD) * SUB
    per_step = (LO + 2 * PAD) // STEPS
    out_step = LO // STEPS

    phase = lax.axis_index("phase")
    bank = lax.axis_index("bank")
    blk = lax.axis_index("blk")
    core = lax.rem(bank, 2)
    chip = bank // 2
    me_sib = (phase, chip * 2 + 1 - core, blk)
    me_next = (1 - phase, bank, blk)
    me_cross = (1 - phase, lax.rem(chip + G // 2, G) * 2 + core, blk)
    up = (phase, bank, lax.rem(blk + 1, Z))
    down = (phase, bank, lax.rem(blk + Z - 1, Z))

    def peer(o):
        return lax.rem(chip + o, G)

    def chip_dev(c):
        return (phase, c * 2 + core, blk)

    barrier = pltpu.get_barrier_semaphore()
    greet = [me_sib, me_next, me_cross, up, down] + [chip_dev(peer(o)) for o in range(1, G)]
    for dev in greet:
        pl.semaphore_signal(
            barrier, inc=1, device_id=dev, device_id_type=pl.DeviceIdType.MESH
        )

    def rc(src, dst, ssem, rsem, dev):
        return pltpu.make_async_remote_copy(
            src_ref=src, dst_ref=dst, send_sem=ssem, recv_sem=rsem,
            device_id=dev, device_id_type=pl.DeviceIdType.MESH,
        )

    mine = pl.ds(pl.multiple_of(core * half_ch, half_ch), half_ch)

    def chip_rows(c):
        return pl.ds(pl.multiple_of(c * ch, ch), ch)

    load_r = pltpu.make_async_copy(rf_ref, rbuf, loc.at[0])
    load_r.start()
    load_m = pltpu.make_async_copy(mw_ref, wmix.at[:, mine], loc.at[1])
    load_m.start()

    lane = lax.broadcasted_iota(jnp.int32, (half_ch, ch), 1)
    row = lax.broadcasted_iota(jnp.int32, (half_ch, ch), 0)
    block = (lane // gw) == (row // gw + core * (half_ch // gw))
    spread = (
        lax.broadcasted_iota(jnp.int32, (gw, ch), 1) % gw
        == lax.broadcasted_iota(jnp.int32, (gw, ch), 0)
    ).astype(F32).astype(BF)
    for l in range(2):
        for k in range(3):
            wide = jnp.dot(cw_ref[l, k], spread, preferred_element_type=F32)
            wconv[l, mine, k * ch : (k + 1) * ch] = jnp.where(block, wide, 0.0).astype(BF)
    move = (
        lax.broadcasted_iota(jnp.int32, (half_ch, ch), 1)
        == lax.broadcasted_iota(jnp.int32, (half_ch, ch), 0) + core * half_ch
    ).astype(F32).astype(BF)
    wown[...] = jnp.dot(pw_ref[...], move, preferred_element_type=F32).astype(BF)

    pl.semaphore_wait(barrier, len(greet))

    first = phase == 0
    second = phase == 1

    c_conv = rc(wconv.at[:, mine], wconv.at[:, mine], sib_s.at[0], sib_r.at[0], me_sib)
    c_mix = rc(mw_ref, wmix.at[:, mine], sib_s.at[1], sib_r.at[1], me_sib)
    c_q = rc(q_ref.at[1 - core], hin.at[mine], sib_s.at[2], sib_r.at[2], me_sib)
    c_h = rc(hout, hin, ph_s.at[0], ph_r.at[0], me_next)
    c_d = rc(D.at[blk, core], D.at[blk, core], ph_s.at[1], ph_r.at[1], me_cross)
    eh = E // 2
    my_e = pl.ds(pl.multiple_of(core * eh, eh), eh)
    its_e = pl.ds(pl.multiple_of((1 - core) * eh, eh), eh)
    c_own = rc(wown.at[its_e], wsib.at[its_e], sib_s.at[3], sib_r.at[3], me_sib)
    c_wp = rc(wproj.at[my_e], wproj.at[my_e], sib_s.at[4], sib_r.at[4], me_sib)

    def chip_cols(c):
        return pl.ds(pl.multiple_of(c * ch, ch), ch)

    def push_proj(o):
        part = wproj.at[my_e, chip_cols(chip)]
        return rc(part, part, gat_s.at[3, o], gat_r.at[3, chip], chip_dev(peer(o)))

    @pl.when(first)
    def _():
        c_q.start()
        hin[mine] = q_ref[core]

    c_conv.start()
    c_mix.start()

    @pl.when(second)
    def _():
        c_own.start()
        c_own.wait_recv()
        wproj[my_e, chip_cols(chip)] = wown[my_e] + wsib[my_e]
        for o in range(1, G):
            push_proj(o).start()

    def gather(l, value):
        U[l, chip_rows(chip)] = value
        for o in range(1, G):
            part = U.at[l, chip_rows(chip)]
            rc(part, part, gat_s.at[l, o], gat_r.at[l, chip], chip_dev(peer(o))).start()
        for o in range(1, G):
            c = peer(o)
            part = U.at[l, chip_rows(c)]
            rc(part, part, gat_s.at[l, o], gat_r.at[l, c], chip_dev(c)).wait_recv()

    def encode():
        @pl.when(first)
        def _():
            c_q.wait_recv()

        @pl.when(second)
        def _():
            c_h.wait_recv()

        c_conv.wait_recv()
        frame = lax.broadcasted_iota(jnp.int32, (ch, T), 1)
        h = hin[...].astype(F32)
        for l in range(2):
            d = jnp.left_shift(jnp.int32(1), phase * 2 + l)
            before = jnp.where(frame >= d, pltpu.roll(h, d, 1), 0.0)
            after = jnp.where(frame < T - d, pltpu.roll(h, T - d, 1), 0.0)
            x = jnp.concatenate([before, h, after], axis=0).astype(BF)
            a = jnp.dot(wconv[l], x, preferred_element_type=F32)
            gather(l, jax.nn.gelu(a, approximate=True).astype(BF))
            if l == 0:
                load_m.wait()
                c_mix.wait_recv()
            u = U[l]
            m = jnp.dot(wmix[l], u, preferred_element_type=F32)
            uf = u.astype(F32)
            sq = jnp.sum(uf * uf, axis=0, keepdims=True)
            h = (h + m * lax.rsqrt(sq / C + 1e-6)).astype(BF).astype(F32)

        @pl.when(first)
        def _():
            hout[...] = h.astype(BF)
            c_h.start()

        @pl.when(second)
        def _():
            gather(2, h.astype(BF))
            c_wp.wait_recv()
            p = jnp.dot(wproj[...], U[2], preferred_element_type=F32)
            norm = lax.rsqrt(jnp.sum(p * p, axis=0, keepdims=True) / E + 1e-6)
            D[blk, core] = (p * norm).astype(BF)
            c_d.start()

    def prepare():
        @pl.when(second)
        def _():
            for o in range(1, G):
                c = peer(o)
                part = wproj.at[my_e, chip_cols(c)]
                rc(part, part, gat_s.at[3, o], gat_r.at[3, c], chip_dev(c)).wait_recv()
            c_wp.start()

        load_r.wait()
        lanes = E // T
        r32[:, 0:8] = jnp.zeros((lanes, 8, T), F32)
        r32[:, F + 8 : F + 16] = jnp.zeros((lanes, 8, T), F32)

        @pl.loop(0, F // 64)
        def _(i):
            at = pl.multiple_of(i * 64, 64)
            for b in range(lanes):
                piece = rbuf[pl.ds(at, 64), b * T : (b + 1) * T]
                r32[b, pl.ds(at + 8, 64)] = piece.astype(F32)

        @pl.loop(0, (LO + 2 * PAD) // 4)
        def _(i):
            for k in range(2):
                at = i * 4 + k * 2 + 8 - PAD
                to = pl.multiple_of(i * 32 + k * 16, 16)
                for b in range(lanes):
                    two = jnp.concatenate(
                        [r32[b, pl.ds(at + v, SUB, stride=LO), :] for v in range(2)], axis=0
                    )
                    rperm[pl.ds(to, 16), b * T : (b + 1) * T] = two.astype(BF)

        ends = []
        total = jnp.int32(0)
        for k in range(slices):
            total = total + sl_ref[0, k]
            ends.append(total)
        scale = E ** (-0.5)

        @pl.loop(0, LO // 8)
        def _(i):
            shape = (8, SUB, T)
            lo = lax.broadcasted_iota(jnp.int32, shape, 0) + i * 8
            r = lax.broadcasted_iota(jnp.int32, shape, 1) * LO + lo
            begin = jnp.zeros(shape, jnp.int32)
            end = jnp.full(shape, F, jnp.int32)
            for e in ends:
                begin = jnp.maximum(begin, jnp.where(r >= e, e, 0))
                end = jnp.minimum(end, jnp.where(r < e, e, F))
            t = (lax.broadcasted_iota(jnp.int32, shape, 2) + lo) & (T - 1)
            at = pl.ds(i * 8, 8)
            for k in range(TAPS):
                j = k - TAPS // 2
                inside = jnp.where((r + j >= begin) & (r + j < end), taps_ref[k] * scale, 0.0)
                wtab[k, at] = jnp.where((t + j >= 0) & (t + j < T), inside, 0.0)

        acc[...] = jnp.full(acc.shape, -jnp.inf, F32)

    @pl.loop(0, 2)
    def _(turn):
        pl.when(turn == phase)(encode)
        pl.when(turn == 0)(prepare)

    @pl.when(first)
    def _():
        c_d.wait_recv()

    def multiply(z, c, into):
        both = jnp.concatenate([D[z, 0], D[z, 1]], axis=1)
        rows = pl.ds(pl.multiple_of(c * (per_step * SUB), 16), per_step * SUB)
        s = jnp.dot(rperm[rows], both, preferred_element_type=F32)
        for i in range(per_step):
            turn = lax.rem(2 * LO + PAD - c * per_step - i, T)
            for n in range(2):
                piece = s[i * SUB : (i + 1) * SUB, n * T : (n + 1) * T]
                into[n, c * per_step + i] = pltpu.roll(piece, turn, 1)

    def select(z, c, s):
        best = [None, None]
        for g in range(out_step // GROUP):
            lo = c * out_step + g * GROUP
            w = [wtab[k, pl.ds(lo, GROUP)] for k in range(TAPS)]
            for n in range(2):
                win = s[n, pl.ds(lo + PAD - 3, GROUP + 6)]
                f = w[0] * win[0:GROUP]
                for k in range(1, TAPS):
                    f = f + w[k] * win[k : k + GROUP]
                f = jnp.max(f, axis=0)
                best[n] = f if best[n] is None else jnp.maximum(best[n], f)
        for n in range(2):
            at = (z * 2 + n) * 2 + c // (STEPS // 2)
            acc[at] = jnp.maximum(acc[at], best[n])

    def run(new, into, old, held):
        @pl.loop(0, STEPS)
        def _(c):
            if old is not None:
                select(old, c, held)
            if new is not None:
                multiply(new, c, into)

    def slot(shift):
        return lax.rem(blk + Z + shift, Z)

    H = Z // 2

    def ring(way, step):
        z = slot((1 - way * 2) * (1 - step))
        ref = D.at[z, core]
        return rc(ref, ref, ring_s.at[way, step], ring_r.at[way, step], (up, down)[way])

    def ring_last(way):
        z = slot((1 - way * 2) * (1 - H))
        ref = D.at[z, core, way * eh : (way + 1) * eh]
        return rc(ref, ref, ring_s.at[way, H], ring_r.at[way, H], (up, down)[way])

    def arrival(way, step):
        ref = D.at[slot((way * 2 - 1) * step), core]
        return rc(ref, ref, ring_s.at[way, step], ring_r.at[way, step], (up, down)[way])

    def arrival_last(way):
        ref = D.at[slot(H), core, way * eh : (way + 1) * eh]
        return rc(ref, ref, ring_s.at[way, H], ring_r.at[way, H], (up, down)[way])

    def hand(z):
        ref = D.at[z, core]
        return rc(ref, ref, sib_s.at[5 + z], sib_r.at[5 + z], me_sib)

    def handed(z):
        ref = D.at[z, 1 - core]
        return rc(ref, ref, sib_s.at[5 + z], sib_r.at[5 + z], me_sib)

    hand(blk).start()
    for way in range(2):
        if H > 1:
            ring(way, 1).start()
        else:
            ring_last(way).start()
    handed(blk).wait_recv()
    run(blk, s1, None, None)

    if H > 1:
        @pl.loop(1, H)
        def _(step):
            for way in range(2):
                arrival(way, step).wait_recv()

                @pl.when(step < H - 1)
                def _():
                    ring(way, step + 1).start()

                @pl.when(step == H - 1)
                def _():
                    ring_last(way).start()

                hand(slot((way * 2 - 1) * step)).start()
            for way in range(2):
                z = slot((way * 2 - 1) * step)
                handed(z).wait_recv()
                prev = slot(-step) if way else slot(step - 1)
                run(z, (s0, s1)[way], prev, (s1, s0)[way])

    for way in range(2):
        arrival_last(way).wait_recv()
    hand(slot(H)).start()
    handed(slot(H)).wait_recv()
    run(slot(H), s0, slot(H - 1), s1)
    run(None, None, slot(H), s0)

    out_ref[...] = jnp.max(
        acc[...].reshape(Z * 4 * SUB, T).T, axis=0, keepdims=True
    )

    c_conv.wait_send()
    c_mix.wait_send()

    @pl.when(first)
    def _():
        c_q.wait_send()
        c_h.wait_send()

    @pl.when(second)
    def _():
        c_own.wait_send()
        c_wp.wait_send()
        c_d.wait_send()
        for o in range(1, G):
            push_proj(o).wait_send()
            part = U.at[2, chip_rows(chip)]
            rc(part, part, gat_s.at[2, o], gat_r.at[2, chip], chip_dev(peer(o))).wait_send()

    for l in range(2):
        for o in range(1, G):
            part = U.at[l, chip_rows(chip)]
            rc(part, part, gat_s.at[l, o], gat_r.at[l, chip], chip_dev(peer(o))).wait_send()
    for way in range(2):
        for step in range(1, H):
            ring(way, step).wait_send()
        ring_last(way).wait_send()
    for z in range(Z):
        hand(z).wait_send()


def solution(mesh):
    G = mesh.shape["bank"] // 2
    Z = mesh.shape["blk"]

    def per_device(q, cw, mw, pw, taps, rf, sl):
        half_ch, T = q.shape[1:]
        ch = 2 * half_ch
        C = mw.shape[2]
        E = pw.shape[0]
        F = rf.shape[0]
        LO = F // SUB
        dma = pltpu.SemaphoreType.DMA
        vmem = pl.BlockSpec(memory_space=pltpu.VMEM)
        smem = pl.BlockSpec(memory_space=pltpu.SMEM)
        anyw = pl.BlockSpec(memory_space=pl.ANY)
        maxima = pl.pallas_call(
            functools.partial(kernel, G, Z),
            out_shape=jax.ShapeDtypeStruct((1, Z * 4 * SUB), F32),
            in_specs=[vmem, vmem, anyw, vmem, smem, anyw, smem],
            out_specs=vmem,
            scratch_shapes=[
                pltpu.VMEM((2, ch, C), BF),
                pltpu.VMEM((2, ch, 3 * ch), BF),
                pltpu.VMEM((E, ch), BF),
                pltpu.VMEM((E, ch), BF),
                pltpu.VMEM((E, C), BF),
                pltpu.VMEM((ch, T), BF),
                pltpu.VMEM((ch, T), BF),
                pltpu.VMEM((3, C, T), BF),
                pltpu.VMEM((Z, 2, E, T), BF),
                pltpu.VMEM((F, E), BF),
                pltpu.VMEM((E // T, F + 16, T), F32),
                pltpu.VMEM(((LO + 2 * PAD) * SUB, E), BF),
                pltpu.VMEM((TAPS, LO, SUB, T), F32),
                pltpu.VMEM((2, LO + 2 * PAD, SUB, T), F32),
                pltpu.VMEM((2, LO + 2 * PAD, SUB, T), F32),
                pltpu.VMEM((Z * 4, SUB, T), F32),
                dma((2,)),
                dma((5 + Z,)),
                dma((5 + Z,)),
                dma((4, G)),
                dma((4, G)),
                dma((2,)),
                dma((2,)),
                dma((2, Z // 2 + 1)),
                dma((2, Z // 2 + 1)),
            ],
            compiler_params=pltpu.CompilerParams(
                collective_id=0,
                has_side_effects=True,
                vmem_limit_bytes=48 * 1024 * 1024,
            ),
        )(q, cw, mw, pw, taps, rf, sl)
        maxima = maxima.reshape(2 * Z, 2, SUB)
        return jnp.transpose(maxima, (0, 2, 1)).reshape(2 * Z, 2 * SUB)

    return jax.shard_map(
        per_device,
        mesh=mesh,
        in_specs=(
            P("blk", "bank", None),
            P("phase", None, "bank", None),
            P("phase", "bank", None),
            P(None, "bank"),
            P(),
            P(("phase", "bank", "blk"), None),
            P(("phase", "bank", "blk"), None),
        ),
        out_specs=P(None, ("phase", "bank", "blk")),
        check_vma=False,
    )
```

```python
import functools

import jax
import jax.numpy as jnp
from jax import lax
from jax.experimental import pallas as pl
from jax.experimental.pallas import tpu as pltpu
from jax.sharding import PartitionSpec as P

BF = jnp.bfloat16
F32 = jnp.float32
TAPS = 7
SUB = 8
PAD = 4
STEPS = 4
GROUP = 8


def kernel(
    G, Z, q_hbm, cw_hbm, mw_ref, pw_hbm, taps_ref, rf_ref, sl_ref, out_ref,
    q_ref, cw_ref, pw_ref, wraw, wconv, wfull, wown, wsib, wproj, hin, hout, hall, U, D,
    rbuf, r32, rperm, wtab, s0, s1, acc,
    loc, sib_s, sib_r, gat_s, gat_r, hop_s, hop_r, par_s, par_r, far_s, far_r, row_s, row_r,
):
    half_ch = q_ref.shape[1]
    ch = 2 * half_ch
    T = q_ref.shape[2]
    C = mw_ref.shape[2]
    E = pw_ref.shape[1]
    F = rf_ref.shape[0]
    slices = sl_ref.shape[1]
    gw = cw_ref.shape[2]
    LO = F // SUB
    per_step = (LO + 2 * PAD) // STEPS
    out_step = LO // STEPS
    Y = G // 2
    H = Z // 2

    phase = lax.axis_index("phase")
    bank = lax.axis_index("bank")
    blk = lax.axis_index("blk")
    core = lax.rem(bank, 2)
    chip = bank // 2
    col = chip // Y
    row = lax.rem(chip, Y)
    me_sib = (phase, chip * 2 + 1 - core, blk)
    across = lax.rem(chip + Y, G) * 2 + core
    first = phase == 0
    second = phase == 1

    def peer(o):
        return lax.rem(chip + o, G)

    def chip_dev(c):
        return (phase, c * 2 + core, blk)

    def row_dev(v):
        return (phase, (col * Y + lax.rem(row + v, Y)) * 2 + core, blk)

    def slot(shift):
        return lax.rem(blk + Z + shift, Z)

    load_q = pltpu.make_async_copy(q_hbm, q_ref, loc.at[2])
    load_c = pltpu.make_async_copy(cw_hbm, cw_ref, loc.at[3])
    load_p = pltpu.make_async_copy(pw_hbm, pw_ref, loc.at[4])
    load_c.start()
    load_q.start()
    load_p.start()

    barrier = pltpu.get_barrier_semaphore()
    greet = [me_sib] + [chip_dev(peer(o)) for o in range(1, G)]
    greet += [(phase, bank, slot(o)) for o in range(1, Z)]
    greet += [(1 - phase, across, slot(o)) for o in range(1, Z)]
    greet += [(1 - phase, c * 2 + core, blk) for c in range(G)]
    for dev in greet:
        pl.semaphore_signal(
            barrier, inc=1, device_id=dev, device_id_type=pl.DeviceIdType.MESH
        )

    load_m = pltpu.make_async_copy(mw_ref, wfull.at[:, chip, core], loc.at[1])
    load_m.start()
    load_r = pltpu.make_async_copy(rf_ref, rbuf, loc.at[0])
    load_r.start()

    def rc(src, dst, ssem, rsem, dev):
        return pltpu.make_async_remote_copy(
            src_ref=src, dst_ref=dst, send_sem=ssem, recv_sem=rsem,
            device_id=dev, device_id_type=pl.DeviceIdType.MESH,
        )

    def iota(shape, axis):
        return lax.broadcasted_iota(jnp.int32, shape, axis)

    def ones(mask):
        return mask.astype(F32).astype(BF)

    def turned(a, b):
        return lax.dot_general(a, b, (((0,), (0,)), ((), ())), preferred_element_type=F32)

    def chip_rows(c):
        return pl.ds(pl.multiple_of(c * ch, ch), ch)

    mine = pl.ds(pl.multiple_of(core * half_ch, half_ch), half_ch)
    eh = E // 2
    my_e = pl.ds(pl.multiple_of(core * eh, eh), eh)
    its_e = pl.ds(pl.multiple_of((1 - core) * eh, eh), eh)
    eq = E // Y

    def part_e(r):
        return pl.ds(pl.multiple_of(r * eq, eq), eq)

    load_c.wait()
    for l in range(2):
        flat = None
        for k in range(3):
            put = ones(iota((gw, T), 1) == iota((gw, T), 0) + k * gw)
            wide = turned(cw_ref[l, k], put)
            flat = wide if flat is None else flat + wide
        wraw[l, chip, core] = flat.astype(BF)
    load_q.wait()

    pl.semaphore_wait(barrier, len(greet))

    c_conv = rc(
        wraw.at[:, chip, core], wraw.at[:, chip, core], sib_s.at[0], sib_r.at[0], me_sib
    )
    c_mix = rc(mw_ref, wfull.at[:, chip, core], sib_s.at[1], sib_r.at[1], me_sib)
    c_q = rc(q_ref.at[1 - core], hin.at[mine], sib_s.at[2], sib_r.at[2], me_sib)
    c_own = rc(wown.at[its_e], wsib.at[its_e], sib_s.at[3], sib_r.at[3], me_sib)
    c_wp = rc(wproj.at[my_e], wproj.at[my_e], sib_s.at[4], sib_r.at[4], me_sib)
    c_conv_all = rc(wraw.at[:, :, core], wraw.at[:, :, core], sib_s.at[5], sib_r.at[5], me_sib)

    def c_mix_all(l):
        return rc(
            wfull.at[l, :, core], wfull.at[l, :, core], sib_s.at[6 + l], sib_r.at[6 + l], me_sib
        )

    def push(kind, o, c):
        if kind == 0:
            src = dst = wraw.at[:, c, core]
        elif kind == 3:
            src = dst = wproj.at[my_e, chip_rows(c)]
        else:
            src, dst = mw_ref.at[kind - 1], wfull.at[kind - 1, c, core]
        return rc(src, dst, par_s.at[kind, o], par_r.at[kind, c], chip_dev(peer(o)))

    spread = ones(
        (iota((T, 3 * ch), 0) // gw == iota((T, 3 * ch), 1) // ch)
        & (iota((T, 3 * ch), 0) % gw == iota((T, 3 * ch), 1) % gw)
    )
    block = iota((ch, 3 * ch), 1) % ch // gw == iota((ch, 3 * ch), 0) // gw

    def expand(raw):
        wide = jnp.dot(raw.reshape(ch, T), spread, preferred_element_type=F32)
        return jnp.where(block, wide, 0.0).astype(BF)

    def shifts(h, d):
        frame = iota(h.shape, 1)
        before = jnp.where(frame >= d, pltpu.roll(h, d, 1), 0.0)
        after = jnp.where(frame < T - d, pltpu.roll(h, T - d, 1), 0.0)
        return before.astype(BF), h.astype(BF), after.astype(BF)

    def mixed(h, w, u):
        m = jnp.dot(w, u, preferred_element_type=F32)
        uf = u.astype(F32)
        sq = jnp.sum(uf * uf, axis=0, keepdims=True)
        return (h + m * lax.rsqrt(sq / C + 1e-6)).astype(BF)

    def encode_first():
        c_q.start()
        c_conv.start()
        c_mix.start()
        hin[mine] = q_ref[core]
        c_q.wait_recv()
        c_conv.wait_recv()
        h = hin[...].astype(F32)
        for l in range(2):
            wide = expand(wraw[l, chip])
            x = jnp.concatenate(shifts(h, 1 << l), axis=0)
            a = jnp.dot(wide, x, preferred_element_type=F32)
            part = U.at[l, chip_rows(chip)]
            part[...] = jax.nn.gelu(a, approximate=True).astype(BF)
            for o in range(1, G):
                rc(part, part, gat_s.at[l, o], gat_r.at[l, chip], chip_dev(peer(o))).start()
            if l == 0:
                load_m.wait()
                c_mix.wait_recv()
            for o in range(1, G):
                c = peer(o)
                other = U.at[l, chip_rows(c)]
                rc(other, other, gat_s.at[l, o], gat_r.at[l, c], chip_dev(c)).wait_recv()
            h = mixed(h, wfull[l, chip].reshape(ch, C), U[l]).astype(F32)
        hout[...] = h.astype(BF)
        for c in range(G):
            hop(c).start()
        load_p.wait()

    def hop(c):
        return rc(hout, hall.at[chip], hop_s.at[c], hop_r.at[chip], (1, c * 2 + core, blk))

    def fetch():
        for kind in range(3):
            for o in range(1, G):
                push(kind, o, chip).start()
        load_p.wait()
        move = ones(iota((half_ch, ch), 1) == iota((half_ch, ch), 0) + core * half_ch)
        wown[...] = turned(pw_ref[...], move).astype(BF)
        c_own.start()
        c_own.wait_recv()
        wproj[my_e, chip_rows(chip)] = wown[my_e] + wsib[my_e]
        for o in range(1, G):
            push(3, o, chip).start()

    def encode_second():
        load_m.wait()
        for kind in range(4):
            for o in range(1, G):
                push(kind, o, peer(o)).wait_recv()
            (c_conv_all, c_mix_all(0), c_mix_all(1), c_wp)[kind].start()
        c_conv_all.wait_recv()
        for l in range(2):
            for c in range(G):
                wconv[l, c] = expand(wraw[l, c])
        for c in range(G):
            rc(hout, hall.at[c], hop_s.at[c], hop_r.at[c], me_sib).wait_recv()
        h = hall[...].reshape(C, T).astype(F32)
        for l in range(2):
            sides = shifts(h, 4 << l)
            for c in range(G):
                x = jnp.concatenate([v[c * ch : (c + 1) * ch] for v in sides], axis=0)
                a = jnp.dot(wconv[l, c], x, preferred_element_type=F32)
                U[l, c * ch : (c + 1) * ch] = jax.nn.gelu(a, approximate=True).astype(BF)
            c_mix_all(l).wait_recv()
            h = mixed(h, wfull[l].reshape(C, C), U[l]).astype(F32)
        c_wp.wait_recv()
        p = jnp.dot(wproj[...], h.astype(BF), preferred_element_type=F32)
        norm = lax.rsqrt(jnp.sum(p * p, axis=0, keepdims=True) / E + 1e-6)
        D[blk, core] = (p * norm).astype(BF)

    def prepare():
        load_r.wait()
        lanes = E // T
        r32[:, 0:8] = jnp.zeros((lanes, 8, T), F32)
        r32[:, F + 8 : F + 16] = jnp.zeros((lanes, 8, T), F32)

        @pl.loop(0, F // 64)
        def _(i):
            at = pl.multiple_of(i * 64, 64)
            for b in range(lanes):
                piece = rbuf[pl.ds(at, 64), b * T : (b + 1) * T]
                r32[b, pl.ds(at + 8, 64)] = piece.astype(F32)

        @pl.loop(0, (LO + 2 * PAD) // 4)
        def _(i):
            for k in range(2):
                at = i * 4 + k * 2 + 8 - PAD
                to = pl.multiple_of(i * 32 + k * 16, 16)
                for b in range(lanes):
                    two = jnp.concatenate(
                        [r32[b, pl.ds(at + v, SUB, stride=LO), :] for v in range(2)], axis=0
                    )
                    rperm[pl.ds(to, 16), b * T : (b + 1) * T] = two.astype(BF)

        ends = []
        total = jnp.int32(0)
        for k in range(slices):
            total = total + sl_ref[0, k]
            ends.append(total)
        scale = E ** (-0.5)

        @pl.loop(0, LO // 8)
        def _(i):
            shape = (8, SUB, T)
            lo = lax.broadcasted_iota(jnp.int32, shape, 0) + i * 8
            r = lax.broadcasted_iota(jnp.int32, shape, 1) * LO + lo
            begin = jnp.zeros(shape, jnp.int32)
            end = jnp.full(shape, F, jnp.int32)
            for e in ends:
                begin = jnp.maximum(begin, jnp.where(r >= e, e, 0))
                end = jnp.minimum(end, jnp.where(r < e, e, F))
            t = (lax.broadcasted_iota(jnp.int32, shape, 2) + lo) & (T - 1)
            at = pl.ds(i * 8, 8)
            for k in range(TAPS):
                j = k - TAPS // 2
                inside = jnp.where((r + j >= begin) & (r + j < end), taps_ref[k] * scale, 0.0)
                wtab[k, at] = jnp.where((t + j >= 0) & (t + j < T), inside, 0.0)

        acc[...] = jnp.full(acc.shape, -jnp.inf, F32)

    def multiply(z, c, into):
        both = jnp.concatenate([D[z, 0], D[z, 1]], axis=1)
        rows = pl.ds(pl.multiple_of(c * (per_step * SUB), 16), per_step * SUB)
        s = jnp.dot(rperm[rows], both, preferred_element_type=F32)
        for i in range(per_step):
            turn = lax.rem(2 * LO + PAD - c * per_step - i, T)
            for n in range(2):
                piece = s[i * SUB : (i + 1) * SUB, n * T : (n + 1) * T]
                into[n, c * per_step + i] = pltpu.roll(piece, turn, 1)

    def select(z, c, s):
        best = [None, None]
        for g in range(out_step // GROUP):
            lo = c * out_step + g * GROUP
            w = [wtab[k, pl.ds(lo, GROUP)] for k in range(TAPS)]
            for n in range(2):
                win = s[n, pl.ds(lo + PAD - 3, GROUP + 6)]
                f = w[0] * win[0:GROUP]
                for k in range(1, TAPS):
                    f = f + w[k] * win[k : k + GROUP]
                f = jnp.max(f, axis=0)
                best[n] = f if best[n] is None else jnp.maximum(best[n], f)
        for n in range(2):
            at = (z * 2 + n) * 2 + c // (STEPS // 2)
            acc[at] = jnp.maximum(acc[at], best[n])

    def run(new, into, old, held):
        @pl.loop(0, STEPS)
        def _(c):
            if old is not None:
                select(old, c, held)
            if new is not None:
                multiply(new, c, into)

    def far(o):
        ref = D.at[blk, core, part_e(row)]
        dev = (phase, bank, slot(o)) if o < Z else (1 - phase, across, slot(o - Z))
        return rc(ref, ref, far_s.at[o], far_r.at[blk], dev)

    def far_from(z):
        ref = D.at[z, core, part_e(row)]
        return rc(ref, ref, far_s.at[0], far_r.at[z], me_sib)

    def along(z, v):
        ref = D.at[z, core, part_e(row)]
        return rc(ref, ref, row_s.at[z, v], row_r.at[z, row], row_dev(v))

    def along_from(z, v):
        r = lax.rem(row + v, Y)
        ref = D.at[z, core, part_e(r)]
        return rc(ref, ref, row_s.at[z, v], row_r.at[z, r], row_dev(v))

    def hand(z):
        ref = D.at[z, core]
        return rc(ref, ref, sib_s.at[8 + z], sib_r.at[8 + z], me_sib)

    def handed(z):
        ref = D.at[z, 1 - core]
        return rc(ref, ref, sib_s.at[8 + z], sib_r.at[8 + z], me_sib)

    def turn(i):
        return slot((i + 1) // 2 * (2 * lax.rem(i, 2) - 1))

    def forward(z):
        far_from(z).wait_recv()
        for v in range(1, Y):
            along(z, v).start()

    def ready(i):
        z = turn(i)
        for v in range(1, Y):
            along_from(z, v).wait_recv()
        hand(z).start()

    pl.when(first)(encode_first)
    pl.when(second)(fetch)
    prepare()
    near = [0] + [w for o in range(1, H + 1) for w in (o, Z - o)][: Z - 1]

    @pl.when(second)
    def _():
        encode_second()
        for o in near:
            if o:
                far(o).start()
            far(Z + o).start()
        hand(blk).start()
        handed(blk).wait_recv()
        run(blk, s1, None, None)

    @pl.when(first)
    def _():
        forward(blk)

    @pl.loop(1, Z)
    def _(i):
        forward(turn(i))

    @pl.when(first)
    def _():
        ready(0)
        handed(blk).wait_recv()
        run(blk, s1, None, None)

    ready(1)

    @pl.loop(0, H - 1)
    def _(g):
        for v in range(2):
            i = 2 * g + 1 + v
            ready(i + 1)
            handed(turn(i)).wait_recv()
            run(turn(i), (s0, s1)[v], turn(i - 1), (s1, s0)[v])

    handed(turn(Z - 1)).wait_recv()
    run(turn(Z - 1), s0, turn(Z - 2), s1)
    run(None, None, turn(Z - 1), s0)

    wide = acc.shape[0] * SUB
    flat = jnp.max(acc[...].reshape(wide, T).T, axis=0, keepdims=True)
    lane = iota((2 * Z, wide), 1)
    apart = jnp.where(lane // (2 * SUB) == iota((2 * Z, wide), 0), flat, 0.0)
    lane = iota((wide, 2 * SUB), 0)
    tile = lane % SUB * 2 + lane // SUB % 2
    pick = (tile == iota((wide, 2 * SUB), 1)).astype(F32)
    out_ref[...] = jnp.dot(
        apart, pick, preferred_element_type=F32, precision=lax.Precision.HIGHEST
    )

    @pl.when(first)
    def _():
        c_conv.wait_send()
        c_mix.wait_send()
        c_q.wait_send()
        for l in range(2):
            for o in range(1, G):
                part = U.at[l, chip_rows(chip)]
                rc(part, part, gat_s.at[l, o], gat_r.at[l, chip], chip_dev(peer(o))).wait_send()
        for c in range(G):
            hop(c).wait_send()
        for v in range(1, Y):
            along(blk, v).wait_send()

    @pl.when(second)
    def _():
        c_own.wait_send()
        c_wp.wait_send()
        c_conv_all.wait_send()
        c_mix_all(0).wait_send()
        c_mix_all(1).wait_send()
        for kind in range(4):
            for o in range(1, G):
                push(kind, o, chip).wait_send()
        for o in range(1, 2 * Z):
            far(o).wait_send()

    for i in range(Z):
        hand(i).wait_send()
    for i in range(1, Z):
        for v in range(1, Y):
            along(slot(i), v).wait_send()


def solution(mesh):
    G = mesh.shape["bank"] // 2
    Z = mesh.shape["blk"]

    def per_device(q, cw, mw, pw, taps, rf, sl):
        half_ch, T = q.shape[1:]
        ch = 2 * half_ch
        C = mw.shape[2]
        E = pw.shape[0]
        F = rf.shape[0]
        LO = F // SUB
        dma = pltpu.SemaphoreType.DMA
        vmem = pl.BlockSpec(memory_space=pltpu.VMEM)
        smem = pl.BlockSpec(memory_space=pltpu.SMEM)
        anyw = pl.BlockSpec(memory_space=pl.ANY)
        cw = jnp.transpose(cw, (0, 1, 3, 2))
        pw = jnp.transpose(pw)
        return pl.pallas_call(
            functools.partial(kernel, G, Z),
            out_shape=jax.ShapeDtypeStruct((2 * Z, 2 * SUB), F32),
            in_specs=[anyw, anyw, anyw, anyw, smem, anyw, smem],
            out_specs=vmem,
            scratch_shapes=[
                pltpu.VMEM(q.shape, BF),
                pltpu.VMEM(cw.shape, BF),
                pltpu.VMEM(pw.shape, BF),
                pltpu.VMEM((2, G, 2, half_ch, T), BF),
                pltpu.VMEM((2, G, ch, 3 * ch), BF),
                pltpu.VMEM((2, G, 2, half_ch, C), BF),
                pltpu.VMEM((E, ch), BF),
                pltpu.VMEM((E, ch), BF),
                pltpu.VMEM((E, C), BF),
                pltpu.VMEM((ch, T), BF),
                pltpu.VMEM((ch, T), BF),
                pltpu.VMEM((G, ch, T), BF),
                pltpu.VMEM((2, C, T), BF),
                pltpu.VMEM((Z, 2, E, T), BF),
                pltpu.VMEM((F, E), BF),
                pltpu.VMEM((E // T, F + 16, T), F32),
                pltpu.VMEM(((LO + 2 * PAD) * SUB, E), BF),
                pltpu.VMEM((TAPS, LO, SUB, T), F32),
                pltpu.VMEM((2, LO + 2 * PAD, SUB, T), F32),
                pltpu.VMEM((2, LO + 2 * PAD, SUB, T), F32),
                pltpu.VMEM((Z * 4, SUB, T), F32),
                dma((5,)),
                dma((8 + Z,)),
                dma((8 + Z,)),
                dma((2, G)),
                dma((2, G)),
                dma((G,)),
                dma((G,)),
                dma((4, G)),
                dma((4, G)),
                dma((2 * Z,)),
                dma((Z,)),
                dma((Z, G // 2)),
                dma((Z, G // 2)),
            ],
            compiler_params=pltpu.CompilerParams(
                collective_id=0,
                has_side_effects=True,
                vmem_limit_bytes=60 * 1024 * 1024,
            ),
        )(q, cw, mw, pw, taps, rf, sl)

    return jax.shard_map(
        per_device,
        mesh=mesh,
        in_specs=(
            P("blk", "bank", None),
            P("phase", None, "bank", None),
            P("phase", "bank", None),
            P(None, "bank"),
            P(),
            P(("phase", "bank", "blk"), None),
            P(("phase", "bank", "blk"), None),
        ),
        out_specs=P(None, ("phase", "bank", "blk")),
        check_vma=False,
    )
```

```python
import functools

import jax
import jax.numpy as jnp
from jax import lax
from jax.experimental import pallas as pl
from jax.experimental.pallas import tpu as pltpu
from jax.sharding import PartitionSpec as P

BF = jnp.bfloat16
F32 = jnp.float32
TAPS = 7
SUB = 8
PAD = 4
STEPS = 4
GROUP = 8
CHUNKS = 4


def kernel(
    G, Z, q_hbm, cw_hbm, mw_ref, pw_hbm, taps_ref, rf_ref, sl_ref, out_ref,
    q_ref, cw_ref, pw_ref, wraw, wconv, wfull, wown, wsib, wproj, hin, hout, hall, h4, U, D,
    rbuf, r32, rperm, wtab, s0, s1, acc,
    loc, sib_s, sib_r, gat_s, gat_r, hop_s, hop_r, par_s, par_r, ring_s, ring_r, cross_s, cross_r,
):
    half_ch = q_ref.shape[1]
    ch = 2 * half_ch
    T = q_ref.shape[2]
    C = mw_ref.shape[2]
    E = pw_ref.shape[1]
    F = rf_ref.shape[0]
    slices = sl_ref.shape[1]
    gw = cw_ref.shape[2]
    LO = F // SUB
    per_step = (LO + 2 * PAD) // STEPS
    out_step = LO // STEPS
    H = Z // 2

    phase = lax.axis_index("phase")
    bank = lax.axis_index("bank")
    blk = lax.axis_index("blk")
    core = lax.rem(bank, 2)
    chip = bank // 2
    me_sib = (phase, chip * 2 + 1 - core, blk)
    across = lax.rem(chip + G // 2, G) * 2 + core
    first = phase == 0
    second = phase == 1

    def peer(o):
        return lax.rem(chip + o, G)

    def chip_dev(c):
        return (phase, c * 2 + core, blk)

    def slot(shift):
        return lax.rem(blk + Z + shift, Z)

    up = (phase, bank, slot(1))
    down = (phase, bank, slot(-1))

    load_q = pltpu.make_async_copy(q_hbm, q_ref, loc.at[2])
    load_c = pltpu.make_async_copy(cw_hbm, cw_ref, loc.at[3])
    load_p = pltpu.make_async_copy(pw_hbm, pw_ref, loc.at[4])
    load_c.start()
    load_q.start()
    load_p.start()

    barrier = pltpu.get_barrier_semaphore()
    greet = [me_sib] + [chip_dev(peer(o)) for o in range(1, G)]
    greet += [up, down]
    greet += [(1 - phase, c * 2 + core, blk) for c in range(G)]
    for dev in greet:
        pl.semaphore_signal(
            barrier, inc=1, device_id=dev, device_id_type=pl.DeviceIdType.MESH
        )

    load_m = pltpu.make_async_copy(mw_ref, wfull.at[:, chip, core], loc.at[1])
    load_m.start()
    load_r = pltpu.make_async_copy(rf_ref, rbuf, loc.at[0])
    load_r.start()

    def rc(src, dst, ssem, rsem, dev):
        return pltpu.make_async_remote_copy(
            src_ref=src, dst_ref=dst, send_sem=ssem, recv_sem=rsem,
            device_id=dev, device_id_type=pl.DeviceIdType.MESH,
        )

    def iota(shape, axis):
        return lax.broadcasted_iota(jnp.int32, shape, axis)

    def ones(mask):
        return mask.astype(F32).astype(BF)

    def turned(a, b):
        return lax.dot_general(a, b, (((0,), (0,)), ((), ())), preferred_element_type=F32)

    def chip_rows(c):
        return pl.ds(pl.multiple_of(c * ch, ch), ch)

    mine = pl.ds(pl.multiple_of(core * half_ch, half_ch), half_ch)
    eh = E // 2
    my_e = pl.ds(pl.multiple_of(core * eh, eh), eh)
    its_e = pl.ds(pl.multiple_of((1 - core) * eh, eh), eh)
    ec = E // CHUNKS
    load_c.wait()
    for l in range(2):
        flat = None
        for k in range(3):
            put = ones(iota((gw, T), 1) == iota((gw, T), 0) + k * gw)
            wide = turned(cw_ref[l, k], put)
            flat = wide if flat is None else flat + wide
        wraw[l, chip, core] = flat.astype(BF)
    load_q.wait()

    pl.semaphore_wait(barrier, len(greet))

    c_conv = rc(
        wraw.at[:, chip, core], wraw.at[:, chip, core], sib_s.at[0], sib_r.at[0], me_sib
    )
    c_mix = rc(mw_ref, wfull.at[:, chip, core], sib_s.at[1], sib_r.at[1], me_sib)
    c_q = rc(q_ref.at[1 - core], hin.at[mine], sib_s.at[2], sib_r.at[2], me_sib)
    c_own = rc(wown.at[its_e], wsib.at[its_e], sib_s.at[3], sib_r.at[3], me_sib)
    c_wp = rc(wproj.at[my_e], wproj.at[my_e], sib_s.at[4], sib_r.at[4], me_sib)
    c_conv_all = rc(wraw.at[:, :, core], wraw.at[:, :, core], sib_s.at[5], sib_r.at[5], me_sib)

    c_mix_all = rc(wfull.at[0, :, core], wfull.at[0, :, core], sib_s.at[6], sib_r.at[6], me_sib)
    c_mix_one = rc(mw_ref.at[1], wfull.at[1, chip, core], sib_s.at[7], sib_r.at[7], me_sib)

    def push(kind, o, c):
        if kind == 0:
            src = dst = wraw.at[:, c, core]
        elif kind == 2:
            src = dst = wproj.at[my_e, chip_rows(c)]
        else:
            src, dst = mw_ref.at[0], wfull.at[0, c, core]
        return rc(src, dst, par_s.at[kind, o], par_r.at[kind, c], chip_dev(peer(o)))

    spread = ones(
        (iota((T, 3 * ch), 0) // gw == iota((T, 3 * ch), 1) // ch)
        & (iota((T, 3 * ch), 0) % gw == iota((T, 3 * ch), 1) % gw)
    )
    block = iota((ch, 3 * ch), 1) % ch // gw == iota((ch, 3 * ch), 0) // gw

    def expand(raw):
        wide = jnp.dot(raw.reshape(ch, T), spread, preferred_element_type=F32)
        return jnp.where(block, wide, 0.0).astype(BF)

    def shifts(h, d):
        frame = iota(h.shape, 1)
        before = jnp.where(frame >= d, pltpu.roll(h, d, 1), 0.0)
        after = jnp.where(frame < T - d, pltpu.roll(h, T - d, 1), 0.0)
        return before.astype(BF), h.astype(BF), after.astype(BF)

    def mixed(h, w, u):
        m = jnp.dot(w, u, preferred_element_type=F32)
        uf = u.astype(F32)
        sq = jnp.sum(uf * uf, axis=0, keepdims=True)
        return (h + m * lax.rsqrt(sq / C + 1e-6)).astype(BF)

    def encode_first():
        c_q.start()
        c_conv.start()
        c_mix.start()
        hin[mine] = q_ref[core]
        c_q.wait_recv()
        c_conv.wait_recv()
        h = hin[...].astype(F32)
        for l in range(2):
            wide = expand(wraw[l, chip])
            x = jnp.concatenate(shifts(h, 1 << l), axis=0)
            a = jnp.dot(wide, x, preferred_element_type=F32)
            part = U.at[l, chip_rows(chip)]
            part[...] = jax.nn.gelu(a, approximate=True).astype(BF)
            for o in range(1, G):
                rc(part, part, gat_s.at[l, o], gat_r.at[l, chip], chip_dev(peer(o))).start()
            if l == 0:
                load_m.wait()
                c_mix.wait_recv()
            for o in range(1, G):
                c = peer(o)
                other = U.at[l, chip_rows(c)]
                rc(other, other, gat_s.at[l, o], gat_r.at[l, c], chip_dev(c)).wait_recv()
            h = mixed(h, wfull[l, chip].reshape(ch, C), U[l]).astype(F32)
        hout[...] = h.astype(BF)
        for c in range(G):
            hop(c).start()
        load_p.wait()

    def hop(c):
        return rc(hout, hall.at[chip], hop_s.at[c], hop_r.at[chip], (1, c * 2 + core, blk))

    def fetch():
        for kind in range(2):
            for o in range(1, G):
                push(kind, o, chip).start()
        c_mix_one.start()
        load_p.wait()
        move = ones(iota((half_ch, ch), 1) == iota((half_ch, ch), 0) + core * half_ch)
        wown[...] = turned(pw_ref[...], move).astype(BF)
        c_own.start()
        c_own.wait_recv()
        wproj[my_e, chip_rows(chip)] = wown[my_e] + wsib[my_e]
        for o in range(1, G):
            push(2, o, chip).start()

    def share4(o, c):
        part = h4.at[chip_rows(c)]
        return rc(part, part, gat_s.at[0, o], gat_r.at[0, c], chip_dev(peer(o)))

    def encode_second():
        load_m.wait()
        for kind, onward in enumerate((c_conv_all, c_mix_all, c_wp)):
            for o in range(1, G):
                push(kind, o, peer(o)).wait_recv()
            onward.start()
        c_conv_all.wait_recv()
        for l in range(2):
            for c in range(G):
                wconv[l, c] = expand(wraw[l, c])
        for c in range(G):
            rc(hout, hall.at[c], hop_s.at[c], hop_r.at[c], me_sib).wait_recv()
        h = hall[...].reshape(C, T).astype(F32)
        for l in range(2):
            sides = shifts(h, 4 << l)
            for c in range(G):
                x = jnp.concatenate([v[c * ch : (c + 1) * ch] for v in sides], axis=0)
                a = jnp.dot(wconv[l, c], x, preferred_element_type=F32)
                U[l, c * ch : (c + 1) * ch] = jax.nn.gelu(a, approximate=True).astype(BF)
            if l == 0:
                c_mix_all.wait_recv()
                hall[...] = mixed(h, wfull[0].reshape(C, C), U[0]).reshape(G, ch, T)
                h = hall[...].reshape(C, T).astype(F32)
        c_mix_one.wait_recv()
        last = mixed(hall[chip].astype(F32), wfull[1, chip].reshape(ch, C), U[1])
        h4[chip_rows(chip)] = last
        for o in range(1, G):
            share4(o, chip).start()
        c_wp.wait_recv()
        for o in range(1, G):
            share4(o, peer(o)).wait_recv()
        p = jnp.dot(wproj[...], h4[...], preferred_element_type=F32)
        norm = lax.rsqrt(jnp.sum(p * p, axis=0, keepdims=True) / E + 1e-6)
        D[blk, core] = (p * norm).astype(BF)

    def prepare():
        load_r.wait()
        lanes = E // T
        r32[:, 0:8] = jnp.zeros((lanes, 8, T), F32)
        r32[:, F + 8 : F + 16] = jnp.zeros((lanes, 8, T), F32)

        @pl.loop(0, F // 64)
        def _(i):
            at = pl.multiple_of(i * 64, 64)
            for b in range(lanes):
                piece = rbuf[pl.ds(at, 64), b * T : (b + 1) * T]
                r32[b, pl.ds(at + 8, 64)] = piece.astype(F32)

        @pl.loop(0, (LO + 2 * PAD) // 4)
        def _(i):
            for k in range(2):
                at = i * 4 + k * 2 + 8 - PAD
                to = pl.multiple_of(i * 32 + k * 16, 16)
                for b in range(lanes):
                    two = jnp.concatenate(
                        [r32[b, pl.ds(at + v, SUB, stride=LO), :] for v in range(2)], axis=0
                    )
                    rperm[pl.ds(to, 16), b * T : (b + 1) * T] = two.astype(BF)

        ends = []
        total = jnp.int32(0)
        for k in range(slices):
            total = total + sl_ref[0, k]
            ends.append(total)
        scale = E ** (-0.5)

        @pl.loop(0, LO // 8)
        def _(i):
            shape = (8, SUB, T)
            lo = lax.broadcasted_iota(jnp.int32, shape, 0) + i * 8
            r = lax.broadcasted_iota(jnp.int32, shape, 1) * LO + lo
            begin = jnp.zeros(shape, jnp.int32)
            end = jnp.full(shape, F, jnp.int32)
            for e in ends:
                begin = jnp.maximum(begin, jnp.where(r >= e, e, 0))
                end = jnp.minimum(end, jnp.where(r < e, e, F))
            t = (lax.broadcasted_iota(jnp.int32, shape, 2) + lo) & (T - 1)
            at = pl.ds(i * 8, 8)
            for k in range(TAPS):
                j = k - TAPS // 2
                inside = jnp.where((r + j >= begin) & (r + j < end), taps_ref[k] * scale, 0.0)
                wtab[k, at] = jnp.where((t + j >= 0) & (t + j < T), inside, 0.0)

        acc[...] = jnp.full(acc.shape, -jnp.inf, F32)

    def multiply(z, c, into):
        both = jnp.concatenate([D[z, 0], D[z, 1]], axis=1)
        rows = pl.ds(pl.multiple_of(c * (per_step * SUB), 16), per_step * SUB)
        s = jnp.dot(rperm[rows], both, preferred_element_type=F32)
        for i in range(per_step):
            turn = lax.rem(2 * LO + PAD - c * per_step - i, T)
            for n in range(2):
                piece = s[i * SUB : (i + 1) * SUB, n * T : (n + 1) * T]
                into[n, c * per_step + i] = pltpu.roll(piece, turn, 1)

    def select(z, c, s):
        best = [None, None]
        for g in range(out_step // GROUP):
            lo = c * out_step + g * GROUP
            w = [wtab[k, pl.ds(lo, GROUP)] for k in range(TAPS)]
            for n in range(2):
                win = s[n, pl.ds(lo + PAD - 3, GROUP + 6)]
                f = w[0] * win[0:GROUP]
                for k in range(1, TAPS):
                    f = f + w[k] * win[k : k + GROUP]
                f = jnp.max(f, axis=0)
                best[n] = f if best[n] is None else jnp.maximum(best[n], f)
        for n in range(2):
            at = (z * 2 + n) * 2 + c // (STEPS // 2)
            acc[at] = jnp.maximum(acc[at], best[n])

    def run(new, into, old, held):
        @pl.loop(0, STEPS)
        def _(c):
            if old is not None:
                select(old, c, held)
            if new is not None:
                multiply(new, c, into)

    def bit(z, k):
        return D.at[z, core, pl.ds(pl.multiple_of(k * ec, ec), ec)]

    def cross(k):
        ref = bit(blk, k)
        return rc(ref, ref, cross_s.at[k], cross_r.at[k], (1 - phase, across, blk))

    def ring(way, step, k):
        ref = bit(slot((1 - way * 2) * (1 - step)), k)
        sems = ring_s.at[way, step, k], ring_r.at[way, step, k]
        return rc(ref, ref, *sems, (up, down)[way])

    def arrival(way, step, k):
        ref = bit(slot((way * 2 - 1) * step), k)
        sems = ring_s.at[way, step, k], ring_r.at[way, step, k]
        return rc(ref, ref, *sems, (up, down)[way])

    def hand(z):
        ref = D.at[z, core]
        return rc(ref, ref, sib_s.at[8 + z], sib_r.at[8 + z], me_sib)

    def handed(z):
        ref = D.at[z, 1 - core]
        return rc(ref, ref, sib_s.at[8 + z], sib_r.at[8 + z], me_sib)

    def order(i):
        return slot((i + 1) // 2 * (1 - 2 * lax.rem(i, 2)))

    half = CHUNKS // 2

    pl.when(first)(encode_first)
    pl.when(second)(fetch)
    prepare()

    @pl.when(second)
    def _():
        encode_second()
        for k in range(CHUNKS):
            cross(k).start()

    for k in range(CHUNKS):
        @pl.when(first)
        def _():
            cross(k).wait_recv()

        for way in range(2):
            ring(way, 1, k).start()
    hand(blk).start()

    @pl.loop(1, H)
    def _(step):
        for k in range(CHUNKS):
            for way in range(2):
                arrival(way, step, k).wait_recv()

                @pl.when((step < H - 1) | (k // half == way))
                def _():
                    ring(way, step + 1, k).start()

        for way in range(2):
            hand(slot((way * 2 - 1) * step)).start()

        @pl.when(step == 1)
        def _():
            handed(blk).wait_recv()
            run(blk, s1, None, None)

        @pl.when(step > 1)
        def _():
            for v in range(2):
                i = 2 * step - 3 + v
                handed(order(i)).wait_recv()
                run(order(i), (s0, s1)[v], order(i - 1), (s1, s0)[v])

    far = order(Z - 1)
    for v in range(2):
        i = Z - 3 + v
        handed(order(i)).wait_recv()
        run(order(i), (s0, s1)[v], order(i - 1), (s1, s0)[v])
        if v == 0:
            for k in range(CHUNKS):
                arrival(k // half, H, k).wait_recv()
            hand(far).start()
    handed(far).wait_recv()
    run(far, s0, order(Z - 2), s1)
    run(None, None, far, s0)

    wide = acc.shape[0] * SUB
    flat = jnp.max(acc[...].reshape(wide, T).T, axis=0, keepdims=True)
    lane = iota((2 * Z, wide), 1)
    apart = jnp.where(lane // (2 * SUB) == iota((2 * Z, wide), 0), flat, 0.0)
    lane = iota((wide, 2 * SUB), 0)
    tile = lane % SUB * 2 + lane // SUB % 2
    pick = (tile == iota((wide, 2 * SUB), 1)).astype(F32)
    out_ref[...] = jnp.dot(
        apart, pick, preferred_element_type=F32, precision=lax.Precision.HIGHEST
    )

    @pl.when(first)
    def _():
        c_conv.wait_send()
        c_mix.wait_send()
        c_q.wait_send()
        for l in range(2):
            for o in range(1, G):
                part = U.at[l, chip_rows(chip)]
                rc(part, part, gat_s.at[l, o], gat_r.at[l, chip], chip_dev(peer(o))).wait_send()
        for c in range(G):
            hop(c).wait_send()

    @pl.when(second)
    def _():
        c_own.wait_send()
        c_wp.wait_send()
        c_conv_all.wait_send()
        c_mix_all.wait_send()
        c_mix_one.wait_send()
        for kind in range(3):
            for o in range(1, G):
                push(kind, o, chip).wait_send()
        for o in range(1, G):
            share4(o, chip).wait_send()
        for k in range(CHUNKS):
            cross(k).wait_send()

    for i in range(Z):
        hand(i).wait_send()
    for k in range(CHUNKS):
        for way in range(2):
            for step in range(1, H):
                ring(way, step, k).wait_send()
        ring(k // half, H, k).wait_send()


def solution(mesh):
    G = mesh.shape["bank"] // 2
    Z = mesh.shape["blk"]

    def per_device(q, cw, mw, pw, taps, rf, sl):
        half_ch, T = q.shape[1:]
        ch = 2 * half_ch
        C = mw.shape[2]
        E = pw.shape[0]
        F = rf.shape[0]
        LO = F // SUB
        dma = pltpu.SemaphoreType.DMA
        vmem = pl.BlockSpec(memory_space=pltpu.VMEM)
        smem = pl.BlockSpec(memory_space=pltpu.SMEM)
        anyw = pl.BlockSpec(memory_space=pl.ANY)
        cw = jnp.transpose(cw, (0, 1, 3, 2))
        pw = jnp.transpose(pw)
        return pl.pallas_call(
            functools.partial(kernel, G, Z),
            out_shape=jax.ShapeDtypeStruct((2 * Z, 2 * SUB), F32),
            in_specs=[anyw, anyw, anyw, anyw, smem, anyw, smem],
            out_specs=vmem,
            scratch_shapes=[
                pltpu.VMEM(q.shape, BF),
                pltpu.VMEM(cw.shape, BF),
                pltpu.VMEM(pw.shape, BF),
                pltpu.VMEM((2, G, 2, half_ch, T), BF),
                pltpu.VMEM((2, G, ch, 3 * ch), BF),
                pltpu.VMEM((2, G, 2, half_ch, C), BF),
                pltpu.VMEM((E, ch), BF),
                pltpu.VMEM((E, ch), BF),
                pltpu.VMEM((E, C), BF),
                pltpu.VMEM((ch, T), BF),
                pltpu.VMEM((ch, T), BF),
                pltpu.VMEM((G, ch, T), BF),
                pltpu.VMEM((C, T), BF),
                pltpu.VMEM((2, C, T), BF),
                pltpu.VMEM((Z, 2, E, T), BF),
                pltpu.VMEM((F, E), BF),
                pltpu.VMEM((E // T, F + 16, T), F32),
                pltpu.VMEM(((LO + 2 * PAD) * SUB, E), BF),
                pltpu.VMEM((TAPS, LO, SUB, T), F32),
                pltpu.VMEM((2, LO + 2 * PAD, SUB, T), F32),
                pltpu.VMEM((2, LO + 2 * PAD, SUB, T), F32),
                pltpu.VMEM((Z * 4, SUB, T), F32),
                dma((5,)),
                dma((8 + Z,)),
                dma((8 + Z,)),
                dma((2, G)),
                dma((2, G)),
                dma((G,)),
                dma((G,)),
                dma((3, G)),
                dma((3, G)),
                dma((2, Z // 2 + 1, CHUNKS)),
                dma((2, Z // 2 + 1, CHUNKS)),
                dma((CHUNKS,)),
                dma((CHUNKS,)),
            ],
            compiler_params=pltpu.CompilerParams(
                collective_id=0,
                has_side_effects=True,
                vmem_limit_bytes=60 * 1024 * 1024,
            ),
        )(q, cw, mw, pw, taps, rf, sl)

    return jax.shard_map(
        per_device,
        mesh=mesh,
        in_specs=(
            P("blk", "bank", None),
            P("phase", None, "bank", None),
            P("phase", "bank", None),
            P(None, "bank"),
            P(),
            P(("phase", "bank", "blk"), None),
            P(("phase", "bank", "blk"), None),
        ),
        out_specs=P(None, ("phase", "bank", "blk")),
        check_vma=False,
    )
```

```python
import functools

import jax
import jax.numpy as jnp
from jax import lax
from jax.experimental import pallas as pl
from jax.experimental.pallas import tpu as pltpu
from jax.sharding import PartitionSpec as P

BF = jnp.bfloat16
F32 = jnp.float32
TAPS = 7
MID = TAPS // 2
SUB = 8
PAD = 4
GROUP = 4
CHUNKS = 4


def kernel(
    G, Z, q_hbm, cw_hbm, mw_ref, pw_hbm, taps_ref, rf_ref, sl_ref, out_ref,
    q_ref, cw_ref, pw_ref, wraw, wconv, wfull, wown, wsib, wproj, hin, hout, hall, h4, U, D,
    rbuf, r32, rperm, wtab, s0, s1, acc,
    loc, sib_s, sib_r, gat_s, gat_r, hop_s, hop_r, par_s, par_r, ring_s, ring_r, cross_s, cross_r,
):
    half_ch = q_ref.shape[1]
    ch = 2 * half_ch
    T = q_ref.shape[2]
    C = mw_ref.shape[2]
    E = pw_ref.shape[1]
    F = rf_ref.shape[0]
    slices = sl_ref.shape[1]
    gw = cw_ref.shape[2]
    LO = F // SUB
    H = Z // 2

    phase = lax.axis_index("phase")
    bank = lax.axis_index("bank")
    blk = lax.axis_index("blk")
    core = lax.rem(bank, 2)
    chip = bank // 2
    me_sib = (phase, chip * 2 + 1 - core, blk)
    across = lax.rem(chip + G // 2, G) * 2 + core
    first = phase == 0
    second = phase == 1

    def peer(o):
        return lax.rem(chip + o, G)

    def chip_dev(c):
        return (phase, c * 2 + core, blk)

    def slot(shift):
        return lax.rem(blk + Z + shift, Z)

    up = (phase, bank, slot(1))
    down = (phase, bank, slot(-1))

    load_q = pltpu.make_async_copy(q_hbm, q_ref, loc.at[2])
    load_c = pltpu.make_async_copy(cw_hbm, cw_ref, loc.at[3])
    load_p = pltpu.make_async_copy(pw_hbm, pw_ref, loc.at[4])
    load_c.start()
    load_q.start()
    load_p.start()

    barrier = pltpu.get_barrier_semaphore()
    greet = [me_sib] + [chip_dev(peer(o)) for o in range(1, G)]
    greet += [up, down]
    greet += [(1 - phase, c * 2 + core, blk) for c in range(G)]
    for dev in greet:
        pl.semaphore_signal(
            barrier, inc=1, device_id=dev, device_id_type=pl.DeviceIdType.MESH
        )

    load_m = pltpu.make_async_copy(mw_ref, wfull.at[:, chip, core], loc.at[1])
    load_m.start()
    load_r = pltpu.make_async_copy(rf_ref, rbuf, loc.at[0])
    load_r.start()

    def rc(src, dst, ssem, rsem, dev):
        return pltpu.make_async_remote_copy(
            src_ref=src, dst_ref=dst, send_sem=ssem, recv_sem=rsem,
            device_id=dev, device_id_type=pl.DeviceIdType.MESH,
        )

    def iota(shape, axis):
        return lax.broadcasted_iota(jnp.int32, shape, axis)

    def ones(mask):
        return mask.astype(F32).astype(BF)

    def turned(a, b):
        return lax.dot_general(a, b, (((0,), (0,)), ((), ())), preferred_element_type=F32)

    def chip_rows(c):
        return pl.ds(pl.multiple_of(c * ch, ch), ch)

    mine = pl.ds(pl.multiple_of(core * half_ch, half_ch), half_ch)
    eh = E // 2
    my_e = pl.ds(pl.multiple_of(core * eh, eh), eh)
    its_e = pl.ds(pl.multiple_of((1 - core) * eh, eh), eh)
    ec = E // CHUNKS
    load_c.wait()
    for l in range(2):
        flat = None
        for k in range(3):
            put = ones(iota((gw, T), 1) == iota((gw, T), 0) + k * gw)
            wide = turned(cw_ref[l, k], put)
            flat = wide if flat is None else flat + wide
        wraw[l, chip, core] = flat.astype(BF)
    load_q.wait()

    pl.semaphore_wait(barrier, len(greet))

    c_conv = rc(
        wraw.at[:, chip, core], wraw.at[:, chip, core], sib_s.at[0], sib_r.at[0], me_sib
    )
    c_mix = rc(mw_ref, wfull.at[:, chip, core], sib_s.at[1], sib_r.at[1], me_sib)
    c_q = rc(q_ref.at[1 - core], hin.at[mine], sib_s.at[2], sib_r.at[2], me_sib)
    c_own = rc(wown.at[its_e], wsib.at[its_e], sib_s.at[3], sib_r.at[3], me_sib)
    c_wp = rc(wproj.at[my_e], wproj.at[my_e], sib_s.at[4], sib_r.at[4], me_sib)
    c_conv_all = rc(wraw.at[:, :, core], wraw.at[:, :, core], sib_s.at[5], sib_r.at[5], me_sib)

    c_mix_all = rc(wfull.at[0, :, core], wfull.at[0, :, core], sib_s.at[6], sib_r.at[6], me_sib)
    c_mix_one = rc(mw_ref.at[1], wfull.at[1, chip, core], sib_s.at[7], sib_r.at[7], me_sib)

    def push(kind, o, c):
        if kind == 0:
            src = dst = wraw.at[:, c, core]
        elif kind == 2:
            src = dst = wproj.at[my_e, chip_rows(c)]
        else:
            src, dst = mw_ref.at[0], wfull.at[0, c, core]
        return rc(src, dst, par_s.at[kind, o], par_r.at[kind, c], chip_dev(peer(o)))

    spread = ones(
        (iota((T, 3 * ch), 0) // gw == iota((T, 3 * ch), 1) // ch)
        & (iota((T, 3 * ch), 0) % gw == iota((T, 3 * ch), 1) % gw)
    )
    block = iota((ch, 3 * ch), 1) % ch // gw == iota((ch, 3 * ch), 0) // gw

    def expand(raw):
        wide = jnp.dot(raw.reshape(ch, T), spread, preferred_element_type=F32)
        return jnp.where(block, wide, 0.0).astype(BF)

    def shifts(h, d):
        frame = iota(h.shape, 1)
        before = jnp.where(frame >= d, pltpu.roll(h, d, 1), 0.0)
        after = jnp.where(frame < T - d, pltpu.roll(h, T - d, 1), 0.0)
        return before.astype(BF), h.astype(BF), after.astype(BF)

    def mixed(h, w, u):
        m = jnp.dot(w, u, preferred_element_type=F32)
        uf = u.astype(F32)
        sq = jnp.sum(uf * uf, axis=0, keepdims=True)
        return (h + m * lax.rsqrt(sq / C + 1e-6)).astype(BF)

    def encode_first():
        c_q.start()
        c_conv.start()
        c_mix.start()
        hin[mine] = q_ref[core]
        c_q.wait_recv()
        c_conv.wait_recv()
        h = hin[...].astype(F32)
        for l in range(2):
            wide = expand(wraw[l, chip])
            x = jnp.concatenate(shifts(h, 1 << l), axis=0)
            a = jnp.dot(wide, x, preferred_element_type=F32)
            part = U.at[l, chip_rows(chip)]
            part[...] = jax.nn.gelu(a, approximate=True).astype(BF)
            for o in range(1, G):
                rc(part, part, gat_s.at[l, o], gat_r.at[l, chip], chip_dev(peer(o))).start()
            if l == 0:
                load_m.wait()
                c_mix.wait_recv()
            for o in range(1, G):
                c = peer(o)
                other = U.at[l, chip_rows(c)]
                rc(other, other, gat_s.at[l, o], gat_r.at[l, c], chip_dev(c)).wait_recv()
            h = mixed(h, wfull[l, chip].reshape(ch, C), U[l]).astype(F32)
        hout[...] = h.astype(BF)
        for c in range(G):
            hop(c).start()
        load_p.wait()

    def hop(c):
        return rc(hout, hall.at[chip], hop_s.at[c], hop_r.at[chip], (1, c * 2 + core, blk))

    def fetch():
        for kind in range(2):
            for o in range(1, G):
                push(kind, o, chip).start()
        c_mix_one.start()
        load_p.wait()
        move = ones(iota((half_ch, ch), 1) == iota((half_ch, ch), 0) + core * half_ch)
        wown[...] = turned(pw_ref[...], move).astype(BF)
        c_own.start()
        c_own.wait_recv()
        wproj[my_e, chip_rows(chip)] = wown[my_e] + wsib[my_e]

    def share4(o, c):
        part = h4.at[chip_rows(c)]
        return rc(part, part, gat_s.at[0, o], gat_r.at[0, c], chip_dev(peer(o)))

    def encode_second():
        load_m.wait()
        for kind, onward in enumerate((c_conv_all, c_mix_all)):
            for o in range(1, G):
                push(kind, o, peer(o)).wait_recv()
            onward.start()
        for o in range(1, G):
            push(2, o, chip).start()
        c_conv_all.wait_recv()
        for l in range(2):
            for c in range(G):
                wconv[l, c] = expand(wraw[l, c])
        for c in range(G):
            rc(hout, hall.at[c], hop_s.at[c], hop_r.at[c], me_sib).wait_recv()
        h = hall[...].reshape(C, T).astype(F32)
        for l in range(2):
            sides = shifts(h, 4 << l)
            for c in range(G):
                x = jnp.concatenate([v[c * ch : (c + 1) * ch] for v in sides], axis=0)
                a = jnp.dot(wconv[l, c], x, preferred_element_type=F32)
                U[l, c * ch : (c + 1) * ch] = jax.nn.gelu(a, approximate=True).astype(BF)
            if l == 0:
                c_mix_all.wait_recv()
                hall[...] = mixed(h, wfull[0].reshape(C, C), U[0]).reshape(G, ch, T)
                h = hall[...].reshape(C, T).astype(F32)
        c_mix_one.wait_recv()
        last = mixed(hall[chip].astype(F32), wfull[1, chip].reshape(ch, C), U[1])
        h4[chip_rows(chip)] = last
        for o in range(1, G):
            share4(o, chip).start()
        for o in range(1, G):
            push(2, o, peer(o)).wait_recv()
        c_wp.start()
        for o in range(1, G):
            share4(o, peer(o)).wait_recv()
        c_wp.wait_recv()
        p = jnp.dot(wproj[...], h4[...], preferred_element_type=F32)
        norm = lax.rsqrt(jnp.sum(p * p, axis=0, keepdims=True) / E + 1e-6)
        D[blk, core] = (p * norm).astype(BF)

    def prepare():
        load_r.wait()
        lanes = E // T
        r32[:, 0:8] = jnp.zeros((lanes, 8, T), F32)
        r32[:, F + 8 : F + 16] = jnp.zeros((lanes, 8, T), F32)

        @pl.loop(0, F // 64)
        def _(i):
            at = pl.multiple_of(i * 64, 64)
            for b in range(lanes):
                piece = rbuf[pl.ds(at, 64), b * T : (b + 1) * T]
                r32[b, pl.ds(at + 8, 64)] = piece.astype(F32)

        @pl.loop(0, (LO + 2 * PAD) // 4)
        def _(i):
            for k in range(2):
                at = i * 4 + k * 2 + 8 - PAD
                to = pl.multiple_of(i * 32 + k * 16, 16)
                for b in range(lanes):
                    two = jnp.concatenate(
                        [r32[b, pl.ds(at + v, SUB, stride=LO), :] for v in range(2)], axis=0
                    )
                    rperm[pl.ds(to, 16), b * T : (b + 1) * T] = two.astype(BF)

        ends = []
        total = jnp.int32(0)
        for k in range(slices):
            total = total + sl_ref[0, k]
            ends.append(total)

        @pl.loop(0, LO // 8)
        def _(i):
            shape = (8, SUB, T)
            lo = lax.broadcasted_iota(jnp.int32, shape, 0) + i * 8
            r = lax.broadcasted_iota(jnp.int32, shape, 1) * LO + lo
            begin = jnp.zeros(shape, jnp.int32)
            end = jnp.full(shape, F, jnp.int32)
            for e in ends:
                begin = jnp.maximum(begin, jnp.where(r >= e, e, 0))
                end = jnp.minimum(end, jnp.where(r < e, e, F))
            t = (lax.broadcasted_iota(jnp.int32, shape, 2) + lo) & (T - 1)
            at = pl.ds(i * 8, 8)
            for k in range(TAPS):
                j = k - MID
                if j == 0:
                    continue
                inside = jnp.where((r + j >= begin) & (r + j < end), taps_ref[k] / taps_ref[MID], 0.0)
                wtab[k, at] = jnp.where((t + j >= 0) & (t + j < T), inside, 0.0)

    def multiply(z, into):
        both = jnp.concatenate([D[z, 0], D[z, 1]], axis=1)
        s = jnp.dot(rperm[...], both, preferred_element_type=F32)
        for i in range(LO + 2 * PAD):
            for n in range(2):
                piece = s[i * SUB : (i + 1) * SUB, n * T : (n + 1) * T]
                into[n, i] = pltpu.roll(piece, (2 * LO + PAD - i) % T, 1)

    def select(z, s):
        for side in range(2):
            best = [None, None]
            for lo in range(side * LO // 2, (side + 1) * LO // 2, GROUP):
                w = [None if k == MID else wtab[k, lo : lo + GROUP] for k in range(TAPS)]
                for n in range(2):
                    win = s[n, lo + PAD - MID : lo + PAD + MID + GROUP]
                    t = [win[k : k + GROUP] for k in range(TAPS)]
                    t = [v if k == MID else w[k] * v for k, v in enumerate(t)]
                    f = (t[0] + t[1]) + (t[2] + t[3]) + (t[4] + t[5] + t[6])
                    f = jnp.max(f, axis=0)
                    best[n] = f if best[n] is None else jnp.maximum(best[n], f)
            for n in range(2):
                acc[(z * 2 + n) * 2 + side] = best[n]

    def run(new, into, old, held):
        if old is not None:
            select(old, held)
        if new is not None:
            multiply(new, into)

    def bit(z, k):
        return D.at[z, core, pl.ds(pl.multiple_of(k * ec, ec), ec)]

    def cross(k):
        ref = bit(blk, k)
        return rc(ref, ref, cross_s.at[k], cross_r.at[k], (1 - phase, across, blk))

    def ring(way, step, k):
        ref = bit(slot((1 - way * 2) * (1 - step)), k)
        sems = ring_s.at[way, step, k], ring_r.at[way, step, k]
        return rc(ref, ref, *sems, (up, down)[way])

    def arrival(way, step, k):
        ref = bit(slot((way * 2 - 1) * step), k)
        sems = ring_s.at[way, step, k], ring_r.at[way, step, k]
        return rc(ref, ref, *sems, (up, down)[way])

    def hand(z):
        ref = D.at[z, core]
        return rc(ref, ref, sib_s.at[8 + z], sib_r.at[8 + z], me_sib)

    def handed(z):
        ref = D.at[z, 1 - core]
        return rc(ref, ref, sib_s.at[8 + z], sib_r.at[8 + z], me_sib)

    def order(i):
        return slot((i + 1) // 2 * (1 - 2 * lax.rem(i, 2)))

    half = CHUNKS // 2
    far = order(Z - 1)

    pl.when(first)(encode_first)
    pl.when(second)(fetch)
    prepare()

    @pl.when(second)
    def _():
        encode_second()
        for k in range(CHUNKS):
            cross(k).start()

    for k in range(CHUNKS):
        @pl.when(first)
        def _():
            cross(k).wait_recv()

        for way in range(2):
            ring(way, 1, k).start()
    hand(blk).start()

    handed(blk).wait_recv()
    run(blk, s1, None, None)

    def relay(step, k):
        for way in range(2):
            arrival(way, step, k).wait_recv()

            @pl.when((step < H - 1) | (k // half == way))
            def _():
                ring(way, step + 1, k).start()

    def hand_both(step):
        for way in range(2):
            hand(slot((way * 2 - 1) * step)).start()

    for k in range(CHUNKS):
        relay(1, k)
    hand_both(1)

    @pl.loop(2, H + 1)
    def _(step):
        for v in range(2):
            i = 2 * step - 3 + v

            @pl.when(step < H)
            def _():
                for k in range(half):
                    relay(step, v * half + k)

            handed(order(i)).wait_recv()
            run(order(i), (s0, s1)[v], order(i - 1), (s1, s0)[v])

            if v == 0:
                @pl.when(step == H)
                def _():
                    for k in range(CHUNKS):
                        arrival(k // half, H, k).wait_recv()
                    hand(far).start()

        @pl.when(step < H)
        def _():
            hand_both(step)

    handed(far).wait_recv()
    run(far, s0, order(Z - 2), s1)
    run(None, None, far, s0)

    wide = acc.shape[0] * SUB
    flat = jnp.max(acc[...].reshape(wide, T).T, axis=0, keepdims=True)
    flat = flat * (taps_ref[MID] * E ** (-0.5))
    lane = iota((2 * Z, wide), 1)
    apart = jnp.where(lane // (2 * SUB) == iota((2 * Z, wide), 0), flat, 0.0)
    lane = iota((wide, 2 * SUB), 0)
    tile = lane % SUB * 2 + lane // SUB % 2
    pick = (tile == iota((wide, 2 * SUB), 1)).astype(F32)
    out_ref[...] = jnp.dot(
        apart, pick, preferred_element_type=F32, precision=lax.Precision.HIGHEST
    )

    @pl.when(first)
    def _():
        c_conv.wait_send()
        c_mix.wait_send()
        c_q.wait_send()
        for l in range(2):
            for o in range(1, G):
                part = U.at[l, chip_rows(chip)]
                rc(part, part, gat_s.at[l, o], gat_r.at[l, chip], chip_dev(peer(o))).wait_send()
        for c in range(G):
            hop(c).wait_send()

    @pl.when(second)
    def _():
        c_own.wait_send()
        c_wp.wait_send()
        c_conv_all.wait_send()
        c_mix_all.wait_send()
        c_mix_one.wait_send()
        for kind in range(3):
            for o in range(1, G):
                push(kind, o, chip).wait_send()
        for o in range(1, G):
            share4(o, chip).wait_send()
        for k in range(CHUNKS):
            cross(k).wait_send()

    for i in range(Z):
        hand(i).wait_send()
    for k in range(CHUNKS):
        for way in range(2):
            for step in range(1, H):
                ring(way, step, k).wait_send()
        ring(k // half, H, k).wait_send()


def solution(mesh):
    G = mesh.shape["bank"] // 2
    Z = mesh.shape["blk"]

    def per_device(q, cw, mw, pw, taps, rf, sl):
        half_ch, T = q.shape[1:]
        ch = 2 * half_ch
        C = mw.shape[2]
        E = pw.shape[0]
        F = rf.shape[0]
        LO = F // SUB
        dma = pltpu.SemaphoreType.DMA
        vmem = pl.BlockSpec(memory_space=pltpu.VMEM)
        smem = pl.BlockSpec(memory_space=pltpu.SMEM)
        anyw = pl.BlockSpec(memory_space=pl.ANY)
        cw = jnp.transpose(cw, (0, 1, 3, 2))
        pw = jnp.transpose(pw)
        return pl.pallas_call(
            functools.partial(kernel, G, Z),
            out_shape=jax.ShapeDtypeStruct((2 * Z, 2 * SUB), F32),
            in_specs=[anyw, anyw, anyw, anyw, smem, anyw, smem],
            out_specs=vmem,
            scratch_shapes=[
                pltpu.VMEM(q.shape, BF),
                pltpu.VMEM(cw.shape, BF),
                pltpu.VMEM(pw.shape, BF),
                pltpu.VMEM((2, G, 2, half_ch, T), BF),
                pltpu.VMEM((2, G, ch, 3 * ch), BF),
                pltpu.VMEM((2, G, 2, half_ch, C), BF),
                pltpu.VMEM((E, ch), BF),
                pltpu.VMEM((E, ch), BF),
                pltpu.VMEM((E, C), BF),
                pltpu.VMEM((ch, T), BF),
                pltpu.VMEM((ch, T), BF),
                pltpu.VMEM((G, ch, T), BF),
                pltpu.VMEM((C, T), BF),
                pltpu.VMEM((2, C, T), BF),
                pltpu.VMEM((Z, 2, E, T), BF),
                pltpu.VMEM((F, E), BF),
                pltpu.VMEM((E // T, F + 16, T), F32),
                pltpu.VMEM(((LO + 2 * PAD) * SUB, E), BF),
                pltpu.VMEM((TAPS, LO, SUB, T), F32),
                pltpu.VMEM((2, LO + 2 * PAD, SUB, T), F32),
                pltpu.VMEM((2, LO + 2 * PAD, SUB, T), F32),
                pltpu.VMEM((Z * 4, SUB, T), F32),
                dma((5,)),
                dma((8 + Z,)),
                dma((8 + Z,)),
                dma((2, G)),
                dma((2, G)),
                dma((G,)),
                dma((G,)),
                dma((3, G)),
                dma((3, G)),
                dma((2, Z // 2 + 1, CHUNKS)),
                dma((2, Z // 2 + 1, CHUNKS)),
                dma((CHUNKS,)),
                dma((CHUNKS,)),
            ],
            compiler_params=pltpu.CompilerParams(
                collective_id=0,
                has_side_effects=True,
                vmem_limit_bytes=60 * 1024 * 1024,
            ),
        )(q, cw, mw, pw, taps, rf, sl)

    return jax.shard_map(
        per_device,
        mesh=mesh,
        in_specs=(
            P("blk", "bank", None),
            P("phase", None, "bank", None),
            P("phase", "bank", None),
            P(None, "bank"),
            P(),
            P(("phase", "bank", "blk"), None),
            P(("phase", "bank", "blk"), None),
        ),
        out_specs=P(None, ("phase", "bank", "blk")),
        check_vma=False,
    )
```

```python
import functools

import jax
import jax.numpy as jnp
from jax import lax
from jax.experimental import pallas as pl
from jax.experimental.pallas import tpu as pltpu
from jax.sharding import PartitionSpec as P

BF = jnp.bfloat16
F32 = jnp.float32
TAPS = 7
MID = TAPS // 2
SUB = 8
PAD = 4
GROUP = 4
CHUNKS = 2


def kernel(
    G, Z, q_hbm, cw_hbm, mw_ref, pw_hbm, taps_ref, rf_ref, sl_ref, out_ref,
    q_ref, cw_ref, pw_ref, wraw, wconv, wfull, wown, wsib, wproj, hin, hout, hall, h4, U, D,
    rbuf, r32, rperm, wtab, s0, s1, acc,
    loc, sib_s, sib_r, gat_s, gat_r, hop_s, hop_r, par_s, par_r, ring_s, ring_r, cross_s, cross_r,
):
    half_ch = q_ref.shape[1]
    ch = 2 * half_ch
    T = q_ref.shape[2]
    C = mw_ref.shape[2]
    E = pw_ref.shape[1]
    F = rf_ref.shape[0]
    slices = sl_ref.shape[1]
    gw = cw_ref.shape[2]
    LO = F // SUB
    H = Z // 2

    phase = lax.axis_index("phase")
    bank = lax.axis_index("bank")
    blk = lax.axis_index("blk")
    core = lax.rem(bank, 2)
    chip = bank // 2
    me_sib = (phase, chip * 2 + 1 - core, blk)
    across = lax.rem(chip + G // 2, G) * 2 + core
    first = phase == 0
    second = phase == 1

    def peer(o):
        return lax.rem(chip + o, G)

    def chip_dev(c):
        return (phase, c * 2 + core, blk)

    def slot(shift):
        return lax.rem(blk + Z + shift, Z)

    up = (phase, bank, slot(1))
    down = (phase, bank, slot(-1))

    load_q = pltpu.make_async_copy(q_hbm, q_ref, loc.at[2])
    load_c = pltpu.make_async_copy(cw_hbm, cw_ref, loc.at[3])
    load_p = pltpu.make_async_copy(pw_hbm, pw_ref, loc.at[4])
    load_c.start()
    load_q.start()
    load_p.start()

    barrier = pltpu.get_barrier_semaphore()
    greet = [me_sib] + [chip_dev(peer(o)) for o in range(1, G)]
    greet += [up, down]
    greet += [(1 - phase, c * 2 + core, blk) for c in range(G)]
    for dev in greet:
        pl.semaphore_signal(
            barrier, inc=1, device_id=dev, device_id_type=pl.DeviceIdType.MESH
        )

    load_m = pltpu.make_async_copy(mw_ref, wfull.at[:, chip, core], loc.at[1])
    load_m.start()
    load_r = pltpu.make_async_copy(rf_ref, rbuf, loc.at[0])
    load_r.start()

    def rc(src, dst, ssem, rsem, dev):
        return pltpu.make_async_remote_copy(
            src_ref=src, dst_ref=dst, send_sem=ssem, recv_sem=rsem,
            device_id=dev, device_id_type=pl.DeviceIdType.MESH,
        )

    def iota(shape, axis):
        return lax.broadcasted_iota(jnp.int32, shape, axis)

    def ones(mask):
        return mask.astype(F32).astype(BF)

    def turned(a, b):
        return lax.dot_general(a, b, (((0,), (0,)), ((), ())), preferred_element_type=F32)

    def chip_rows(c):
        return pl.ds(pl.multiple_of(c * ch, ch), ch)

    mine = pl.ds(pl.multiple_of(core * half_ch, half_ch), half_ch)
    eh = E // 2
    my_e = pl.ds(pl.multiple_of(core * eh, eh), eh)
    its_e = pl.ds(pl.multiple_of((1 - core) * eh, eh), eh)
    ec = E // CHUNKS
    load_c.wait()
    for l in range(2):
        flat = None
        for k in range(3):
            put = ones(iota((gw, T), 1) == iota((gw, T), 0) + k * gw)
            wide = turned(cw_ref[l, k], put)
            flat = wide if flat is None else flat + wide
        wraw[l, chip, core] = flat.astype(BF)
    load_q.wait()

    pl.semaphore_wait(barrier, len(greet))

    c_conv = rc(
        wraw.at[:, chip, core], wraw.at[:, chip, core], sib_s.at[0], sib_r.at[0], me_sib
    )
    c_mix = rc(mw_ref, wfull.at[:, chip, core], sib_s.at[1], sib_r.at[1], me_sib)
    c_q = rc(q_ref.at[1 - core], hin.at[mine], sib_s.at[2], sib_r.at[2], me_sib)
    c_own = rc(wown.at[its_e], wsib.at[its_e], sib_s.at[3], sib_r.at[3], me_sib)
    c_wp = rc(wproj.at[my_e], wproj.at[my_e], sib_s.at[4], sib_r.at[4], me_sib)
    c_conv_all = rc(wraw.at[:, :, core], wraw.at[:, :, core], sib_s.at[5], sib_r.at[5], me_sib)

    c_mix_all = rc(wfull.at[0, :, core], wfull.at[0, :, core], sib_s.at[6], sib_r.at[6], me_sib)
    c_mix_one = rc(mw_ref.at[1], wfull.at[1, chip, core], sib_s.at[7], sib_r.at[7], me_sib)

    def push(kind, o, c):
        if kind == 0:
            src = dst = wraw.at[:, c, core]
        elif kind == 2:
            src = dst = wproj.at[my_e, chip_rows(c)]
        else:
            src, dst = mw_ref.at[0], wfull.at[0, c, core]
        return rc(src, dst, par_s.at[kind, o], par_r.at[kind, c], chip_dev(peer(o)))

    spread = ones(
        (iota((T, 3 * ch), 0) // gw == iota((T, 3 * ch), 1) // ch)
        & (iota((T, 3 * ch), 0) % gw == iota((T, 3 * ch), 1) % gw)
    )
    block = iota((ch, 3 * ch), 1) % ch // gw == iota((ch, 3 * ch), 0) // gw

    def expand(raw):
        wide = jnp.dot(raw.reshape(ch, T), spread, preferred_element_type=F32)
        return jnp.where(block, wide, 0.0).astype(BF)

    def shifts(h, d):
        frame = iota(h.shape, 1)
        before = jnp.where(frame >= d, pltpu.roll(h, d, 1), 0.0)
        after = jnp.where(frame < T - d, pltpu.roll(h, T - d, 1), 0.0)
        return before.astype(BF), h.astype(BF), after.astype(BF)

    def mixed(h, w, u):
        m = jnp.dot(w, u, preferred_element_type=F32)
        uf = u.astype(F32)
        sq = jnp.sum(uf * uf, axis=0, keepdims=True)
        return (h + m * lax.rsqrt(sq / C + 1e-6)).astype(BF)

    def encode_first():
        c_q.start()
        c_conv.start()
        c_mix.start()
        hin[mine] = q_ref[core]
        c_q.wait_recv()
        c_conv.wait_recv()
        h = hin[...].astype(F32)
        wide = expand(wraw[0, chip])
        for l in range(2):
            x = jnp.concatenate(shifts(h, 1 << l), axis=0)
            a = jnp.dot(wide, x, preferred_element_type=F32)
            part = U.at[l, chip_rows(chip)]
            part[...] = jax.nn.gelu(a, approximate=True).astype(BF)
            for o in range(1, G):
                rc(part, part, gat_s.at[l, o], gat_r.at[l, chip], chip_dev(peer(o))).start()
            if l == 0:
                wide = expand(wraw[1, chip])
                load_m.wait()
                c_mix.wait_recv()
            for o in range(1, G):
                c = peer(o)
                other = U.at[l, chip_rows(c)]
                rc(other, other, gat_s.at[l, o], gat_r.at[l, c], chip_dev(c)).wait_recv()
            h = mixed(h, wfull[l, chip].reshape(ch, C), U[l]).astype(F32)
        hout[...] = h.astype(BF)
        for c in range(G):
            hop(c).start()
        load_p.wait()

    def hop(c):
        return rc(hout, hall.at[chip], hop_s.at[c], hop_r.at[chip], (1, c * 2 + core, blk))

    def fetch():
        for kind in range(2):
            for o in range(1, G):
                push(kind, o, chip).start()
        c_mix_one.start()
        load_p.wait()
        move = ones(iota((half_ch, ch), 1) == iota((half_ch, ch), 0) + core * half_ch)
        wown[...] = turned(pw_ref[...], move).astype(BF)
        c_own.start()
        c_own.wait_recv()
        wproj[my_e, chip_rows(chip)] = wown[my_e] + wsib[my_e]

    def share4(o, c):
        part = h4.at[chip_rows(c)]
        return rc(part, part, gat_s.at[0, o], gat_r.at[0, c], chip_dev(peer(o)))

    def encode_second():
        load_m.wait()
        for kind, onward in enumerate((c_conv_all, c_mix_all)):
            for o in range(1, G):
                push(kind, o, peer(o)).wait_recv()
            onward.start()
        for o in range(1, G):
            push(2, o, chip).start()
        c_conv_all.wait_recv()
        for l in range(2):
            for c in range(G):
                wconv[l, c] = expand(wraw[l, c])
        for c in range(G):
            rc(hout, hall.at[c], hop_s.at[c], hop_r.at[c], me_sib).wait_recv()
        h = hall[...].reshape(C, T).astype(F32)
        for l in range(2):
            sides = shifts(h, 4 << l)
            for c in range(G):
                x = jnp.concatenate([v[c * ch : (c + 1) * ch] for v in sides], axis=0)
                a = jnp.dot(wconv[l, c], x, preferred_element_type=F32)
                U[l, c * ch : (c + 1) * ch] = jax.nn.gelu(a, approximate=True).astype(BF)
            if l == 0:
                c_mix_all.wait_recv()
                hall[...] = mixed(h, wfull[0].reshape(C, C), U[0]).reshape(G, ch, T)
                h = hall[...].reshape(C, T).astype(F32)
        c_mix_one.wait_recv()
        last = mixed(hall[chip].astype(F32), wfull[1, chip].reshape(ch, C), U[1])
        h4[chip_rows(chip)] = last
        for o in range(1, G):
            share4(o, chip).start()
        for o in range(1, G):
            push(2, o, peer(o)).wait_recv()
        c_wp.start()
        for o in range(1, G):
            share4(o, peer(o)).wait_recv()
        c_wp.wait_recv()
        p = jnp.dot(wproj[...], h4[...], preferred_element_type=F32)
        norm = lax.rsqrt(jnp.sum(p * p, axis=0, keepdims=True) / E + 1e-6)
        D[blk, core] = (p * norm).astype(BF)

    def prepare():
        load_r.wait()
        lanes = E // T
        r32[:, 0:8] = jnp.zeros((lanes, 8, T), F32)
        r32[:, F + 8 : F + 16] = jnp.zeros((lanes, 8, T), F32)

        @pl.loop(0, F // 64)
        def _(i):
            at = pl.multiple_of(i * 64, 64)
            for b in range(lanes):
                piece = rbuf[pl.ds(at, 64), b * T : (b + 1) * T]
                r32[b, pl.ds(at + 8, 64)] = piece.astype(F32)

        @pl.loop(0, (LO + 2 * PAD) // 4)
        def _(i):
            for k in range(2):
                at = i * 4 + k * 2 + 8 - PAD
                to = pl.multiple_of(i * 32 + k * 16, 16)
                for b in range(lanes):
                    two = jnp.concatenate(
                        [r32[b, pl.ds(at + v, SUB, stride=LO), :] for v in range(2)], axis=0
                    )
                    rperm[pl.ds(to, 16), b * T : (b + 1) * T] = two.astype(BF)

        ends = []
        total = jnp.int32(0)
        for k in range(slices):
            total = total + sl_ref[0, k]
            ends.append(total)

        @pl.loop(0, LO // 8)
        def _(i):
            shape = (8, SUB, T)
            lo = lax.broadcasted_iota(jnp.int32, shape, 0) + i * 8
            r = lax.broadcasted_iota(jnp.int32, shape, 1) * LO + lo
            begin = jnp.zeros(shape, jnp.int32)
            end = jnp.full(shape, F, jnp.int32)
            for e in ends:
                begin = jnp.maximum(begin, jnp.where(r >= e, e, 0))
                end = jnp.minimum(end, jnp.where(r < e, e, F))
            t = (lax.broadcasted_iota(jnp.int32, shape, 2) + lo) & (T - 1)
            at = pl.ds(i * 8, 8)
            for k in range(TAPS):
                j = k - MID
                if j == 0:
                    continue
                inside = jnp.where((r + j >= begin) & (r + j < end), taps_ref[k] / taps_ref[MID], 0.0)
                wtab[k, at] = jnp.where((t + j >= 0) & (t + j < T), inside, 0.0)

    def multiply(z, into):
        both = jnp.concatenate([D[z, 0], D[z, 1]], axis=1)
        s = jnp.dot(rperm[...], both, preferred_element_type=F32)
        for i in range(LO + 2 * PAD):
            for n in range(2):
                piece = s[i * SUB : (i + 1) * SUB, n * T : (n + 1) * T]
                into[n, i] = pltpu.roll(piece, (2 * LO + PAD - i) % T, 1)

    def select(z, s):
        for side in range(2):
            best = [None, None]
            for lo in range(side * LO // 2, (side + 1) * LO // 2, GROUP):
                w = [None if k == MID else wtab[k, lo : lo + GROUP] for k in range(TAPS)]
                for n in range(2):
                    win = s[n, lo + PAD - MID : lo + PAD + MID + GROUP]
                    t = [win[k : k + GROUP] for k in range(TAPS)]
                    t = [v if k == MID else w[k] * v for k, v in enumerate(t)]
                    f = (t[0] + t[1]) + (t[2] + t[3]) + (t[4] + t[5] + t[6])
                    f = jnp.max(f, axis=0)
                    best[n] = f if best[n] is None else jnp.maximum(best[n], f)
            for n in range(2):
                acc[(z * 2 + n) * 2 + side] = best[n]

    def run(new, into, old, held):
        if old is not None:
            select(old, held)
        if new is not None:
            multiply(new, into)

    def bit(z, k):
        return D.at[z, core, pl.ds(pl.multiple_of(k * ec, ec), ec)]

    def cross(k):
        ref = bit(blk, k)
        return rc(ref, ref, cross_s.at[k], cross_r.at[k], (1 - phase, across, blk))

    def ring(way, step, k):
        ref = bit(slot((1 - way * 2) * (1 - step)), k)
        sems = ring_s.at[way, step, k], ring_r.at[way, step, k]
        return rc(ref, ref, *sems, (up, down)[way])

    def arrival(way, step, k):
        ref = bit(slot((way * 2 - 1) * step), k)
        sems = ring_s.at[way, step, k], ring_r.at[way, step, k]
        return rc(ref, ref, *sems, (up, down)[way])

    def hand(z):
        ref = D.at[z, core]
        return rc(ref, ref, sib_s.at[8 + z], sib_r.at[8 + z], me_sib)

    def handed(z):
        ref = D.at[z, 1 - core]
        return rc(ref, ref, sib_s.at[8 + z], sib_r.at[8 + z], me_sib)

    def order(i):
        return slot((i + 1) // 2 * (1 - 2 * lax.rem(i, 2)))

    half = CHUNKS // 2
    far = order(Z - 1)

    pl.when(first)(encode_first)
    pl.when(second)(fetch)
    prepare()

    @pl.when(second)
    def _():
        encode_second()
        for k in range(CHUNKS):
            cross(k).start()

    for k in range(CHUNKS):
        @pl.when(first)
        def _():
            cross(k).wait_recv()

        for way in range(2):
            ring(way, 1, k).start()
    hand(blk).start()

    handed(blk).wait_recv()
    run(blk, s1, None, None)

    def relay(step, k):
        for way in range(2):
            arrival(way, step, k).wait_recv()

            @pl.when((step < H - 1) | (k // half == way))
            def _():
                ring(way, step + 1, k).start()

    def hand_both(step):
        for way in range(2):
            hand(slot((way * 2 - 1) * step)).start()

    for k in range(CHUNKS):
        relay(1, k)
    hand_both(1)

    @pl.loop(2, H + 1)
    def _(step):
        @pl.when(step < H)
        def _():
            for k in range(CHUNKS):
                relay(step, k)
            hand_both(step)

        for v in range(2):
            i = 2 * step - 3 + v
            handed(order(i)).wait_recv()
            run(order(i), (s0, s1)[v], order(i - 1), (s1, s0)[v])

            if v == 0:
                @pl.when(step == H)
                def _():
                    for k in range(CHUNKS):
                        arrival(k // half, H, k).wait_recv()
                    hand(far).start()

    handed(far).wait_recv()
    run(far, s0, order(Z - 2), s1)
    run(None, None, far, s0)

    wide = acc.shape[0] * SUB
    flat = jnp.max(acc[...].reshape(wide, T).T, axis=0, keepdims=True)
    flat = flat * (taps_ref[MID] * E ** (-0.5))
    lane = iota((2 * Z, wide), 1)
    apart = jnp.where(lane // (2 * SUB) == iota((2 * Z, wide), 0), flat, 0.0)
    lane = iota((wide, 2 * SUB), 0)
    tile = lane % SUB * 2 + lane // SUB % 2
    pick = (tile == iota((wide, 2 * SUB), 1)).astype(F32)
    out_ref[...] = jnp.dot(
        apart, pick, preferred_element_type=F32, precision=lax.Precision.HIGHEST
    )

    @pl.when(first)
    def _():
        c_conv.wait_send()
        c_mix.wait_send()
        c_q.wait_send()
        for l in range(2):
            for o in range(1, G):
                part = U.at[l, chip_rows(chip)]
                rc(part, part, gat_s.at[l, o], gat_r.at[l, chip], chip_dev(peer(o))).wait_send()
        for c in range(G):
            hop(c).wait_send()

    @pl.when(second)
    def _():
        c_own.wait_send()
        c_wp.wait_send()
        c_conv_all.wait_send()
        c_mix_all.wait_send()
        c_mix_one.wait_send()
        for kind in range(3):
            for o in range(1, G):
                push(kind, o, chip).wait_send()
        for o in range(1, G):
            share4(o, chip).wait_send()
        for k in range(CHUNKS):
            cross(k).wait_send()

    for i in range(Z):
        hand(i).wait_send()
    for k in range(CHUNKS):
        for way in range(2):
            for step in range(1, H):
                ring(way, step, k).wait_send()
        ring(k // half, H, k).wait_send()


def solution(mesh):
    G = mesh.shape["bank"] // 2
    Z = mesh.shape["blk"]

    def per_device(q, cw, mw, pw, taps, rf, sl):
        half_ch, T = q.shape[1:]
        ch = 2 * half_ch
        C = mw.shape[2]
        E = pw.shape[0]
        F = rf.shape[0]
        LO = F // SUB
        dma = pltpu.SemaphoreType.DMA
        vmem = pl.BlockSpec(memory_space=pltpu.VMEM)
        smem = pl.BlockSpec(memory_space=pltpu.SMEM)
        anyw = pl.BlockSpec(memory_space=pl.ANY)
        cw = jnp.transpose(cw, (0, 1, 3, 2))
        pw = jnp.transpose(pw)
        return pl.pallas_call(
            functools.partial(kernel, G, Z),
            out_shape=jax.ShapeDtypeStruct((2 * Z, 2 * SUB), F32),
            in_specs=[anyw, anyw, anyw, anyw, smem, anyw, smem],
            out_specs=vmem,
            scratch_shapes=[
                pltpu.VMEM(q.shape, BF),
                pltpu.VMEM(cw.shape, BF),
                pltpu.VMEM(pw.shape, BF),
                pltpu.VMEM((2, G, 2, half_ch, T), BF),
                pltpu.VMEM((2, G, ch, 3 * ch), BF),
                pltpu.VMEM((2, G, 2, half_ch, C), BF),
                pltpu.VMEM((E, ch), BF),
                pltpu.VMEM((E, ch), BF),
                pltpu.VMEM((E, C), BF),
                pltpu.VMEM((ch, T), BF),
                pltpu.VMEM((ch, T), BF),
                pltpu.VMEM((G, ch, T), BF),
                pltpu.VMEM((C, T), BF),
                pltpu.VMEM((2, C, T), BF),
                pltpu.VMEM((Z, 2, E, T), BF),
                pltpu.VMEM((F, E), BF),
                pltpu.VMEM((E // T, F + 16, T), F32),
                pltpu.VMEM(((LO + 2 * PAD) * SUB, E), BF),
                pltpu.VMEM((TAPS, LO, SUB, T), F32),
                pltpu.VMEM((2, LO + 2 * PAD, SUB, T), F32),
                pltpu.VMEM((2, LO + 2 * PAD, SUB, T), F32),
                pltpu.VMEM((Z * 4, SUB, T), F32),
                dma((5,)),
                dma((8 + Z,)),
                dma((8 + Z,)),
                dma((2, G)),
                dma((2, G)),
                dma((G,)),
                dma((G,)),
                dma((3, G)),
                dma((3, G)),
                dma((2, Z // 2 + 1, CHUNKS)),
                dma((2, Z // 2 + 1, CHUNKS)),
                dma((CHUNKS,)),
                dma((CHUNKS,)),
            ],
            compiler_params=pltpu.CompilerParams(
                collective_id=0,
                has_side_effects=True,
                vmem_limit_bytes=60 * 1024 * 1024,
            ),
        )(q, cw, mw, pw, taps, rf, sl)

    return jax.shard_map(
        per_device,
        mesh=mesh,
        in_specs=(
            P("blk", "bank", None),
            P("phase", None, "bank", None),
            P("phase", "bank", None),
            P(None, "bank"),
            P(),
            P(("phase", "bank", "blk"), None),
            P(("phase", "bank", "blk"), None),
        ),
        out_specs=P(None, ("phase", "bank", "blk")),
        check_vma=False,
    )
```

```python
import functools

import jax
import jax.numpy as jnp
from jax import lax
from jax.experimental import pallas as pl
from jax.experimental.pallas import tpu as pltpu
from jax.sharding import PartitionSpec as P

BF = jnp.bfloat16
F32 = jnp.float32
TAPS = 7
MID = TAPS // 2
SUB = 8
PAD = 4
GROUP = 4
CHUNKS = 2


def kernel(
    G, Z, q_hbm, cw_hbm, mw_ref, pw_hbm, taps_ref, rf_ref, sl_ref, out_ref,
    q_ref, cw_ref, pw_ref, wraw, wconv, wfull, wown, wsib, wproj, hin, hout, hall, h4, U, D,
    rbuf, r32, rperm, wtab, s0, s1, acc,
    loc, sib_s, sib_r, gat_s, gat_r, hop_s, hop_r, par_s, par_r, ring_s, ring_r, cross_s, cross_r,
):
    half_ch = q_ref.shape[1]
    ch = 2 * half_ch
    T = q_ref.shape[2]
    C = mw_ref.shape[2]
    E = pw_ref.shape[1]
    F = rf_ref.shape[0]
    slices = sl_ref.shape[1]
    gw = cw_ref.shape[2]
    LO = F // SUB
    H = Z // 2

    phase = lax.axis_index("phase")
    bank = lax.axis_index("bank")
    blk = lax.axis_index("blk")
    core = lax.rem(bank, 2)
    chip = bank // 2
    me_sib = (phase, chip * 2 + 1 - core, blk)
    across = lax.rem(chip + G // 2, G) * 2 + core
    first = phase == 0
    second = phase == 1

    def peer(o):
        return lax.rem(chip + o, G)

    def chip_dev(c):
        return (phase, c * 2 + core, blk)

    def slot(shift):
        return lax.rem(blk + Z + shift, Z)

    up = (phase, bank, slot(1))
    down = (phase, bank, slot(-1))

    load_q = pltpu.make_async_copy(q_hbm, q_ref, loc.at[2])
    load_c = pltpu.make_async_copy(cw_hbm, cw_ref, loc.at[3])
    load_p = pltpu.make_async_copy(pw_hbm, pw_ref, loc.at[4])
    load_c.start()
    load_q.start()
    load_p.start()

    barrier = pltpu.get_barrier_semaphore()
    greet = [me_sib] + [chip_dev(peer(o)) for o in range(1, G)]
    greet += [up, down]
    greet += [(1 - phase, c * 2 + core, blk) for c in range(G)]
    for dev in greet:
        pl.semaphore_signal(
            barrier, inc=1, device_id=dev, device_id_type=pl.DeviceIdType.MESH
        )

    load_m = pltpu.make_async_copy(mw_ref, wfull.at[:, chip, core], loc.at[1])
    load_m.start()
    load_r = pltpu.make_async_copy(rf_ref, rbuf, loc.at[0])
    load_r.start()

    def rc(src, dst, ssem, rsem, dev):
        return pltpu.make_async_remote_copy(
            src_ref=src, dst_ref=dst, send_sem=ssem, recv_sem=rsem,
            device_id=dev, device_id_type=pl.DeviceIdType.MESH,
        )

    def iota(shape, axis):
        return lax.broadcasted_iota(jnp.int32, shape, axis)

    def ones(mask):
        return mask.astype(F32).astype(BF)

    def turned(a, b):
        return lax.dot_general(a, b, (((0,), (0,)), ((), ())), preferred_element_type=F32)

    def chip_rows(c):
        return pl.ds(pl.multiple_of(c * ch, ch), ch)

    mine = pl.ds(pl.multiple_of(core * half_ch, half_ch), half_ch)
    eh = E // 2
    my_e = pl.ds(pl.multiple_of(core * eh, eh), eh)
    its_e = pl.ds(pl.multiple_of((1 - core) * eh, eh), eh)
    ec = E // CHUNKS
    load_c.wait()
    for l in range(2):
        flat = None
        for k in range(3):
            put = ones(iota((gw, T), 1) == iota((gw, T), 0) + k * gw)
            wide = turned(cw_ref[l, k], put)
            flat = wide if flat is None else flat + wide
        wraw[l, chip, core] = flat.astype(BF)
    load_q.wait()

    pl.semaphore_wait(barrier, len(greet))

    c_conv = rc(
        wraw.at[:, chip, core], wraw.at[:, chip, core], sib_s.at[0], sib_r.at[0], me_sib
    )
    c_mix = rc(mw_ref, wfull.at[:, chip, core], sib_s.at[1], sib_r.at[1], me_sib)
    c_q = rc(q_ref.at[1 - core], hin.at[mine], sib_s.at[2], sib_r.at[2], me_sib)
    c_own = rc(wown.at[its_e], wsib.at[its_e], sib_s.at[3], sib_r.at[3], me_sib)
    c_wp = rc(wproj.at[my_e], wproj.at[my_e], sib_s.at[4], sib_r.at[4], me_sib)
    c_conv_all = rc(wraw.at[:, :, core], wraw.at[:, :, core], sib_s.at[5], sib_r.at[5], me_sib)

    c_mix_all = rc(wfull.at[0, :, core], wfull.at[0, :, core], sib_s.at[6], sib_r.at[6], me_sib)
    c_mix_one = rc(mw_ref.at[1], wfull.at[1, chip, core], sib_s.at[7], sib_r.at[7], me_sib)

    def push(kind, o, c):
        if kind == 0:
            src = dst = wraw.at[:, c, core]
        elif kind == 2:
            src = dst = wproj.at[my_e, chip_rows(c)]
        else:
            src, dst = mw_ref.at[0], wfull.at[0, c, core]
        return rc(src, dst, par_s.at[kind, o], par_r.at[kind, c], chip_dev(peer(o)))

    spread = ones(
        (iota((T, 3 * ch), 0) // gw == iota((T, 3 * ch), 1) // ch)
        & (iota((T, 3 * ch), 0) % gw == iota((T, 3 * ch), 1) % gw)
    )
    block = iota((ch, 3 * ch), 1) % ch // gw == iota((ch, 3 * ch), 0) // gw

    def expand(raw):
        wide = jnp.dot(raw.reshape(ch, T), spread, preferred_element_type=F32)
        return jnp.where(block, wide, 0.0).astype(BF)

    def shifts(h, d):
        frame = iota(h.shape, 1)
        before = jnp.where(frame >= d, pltpu.roll(h, d, 1), 0.0)
        after = jnp.where(frame < T - d, pltpu.roll(h, T - d, 1), 0.0)
        return before.astype(BF), h.astype(BF), after.astype(BF)

    def mixed(h, w, u):
        m = jnp.dot(w, u, preferred_element_type=F32)
        uf = u.astype(F32)
        sq = jnp.sum(uf * uf, axis=0, keepdims=True)
        return (h + m * lax.rsqrt(sq / C + 1e-6)).astype(BF)

    def encode_first():
        c_q.start()
        c_conv.start()
        hin[mine] = q_ref[core]
        c_conv.wait_recv()
        wide = expand(wraw[0, chip])
        c_q.wait_recv()
        c_mix.start()
        h = hin[...].astype(F32)
        for l in range(2):
            x = jnp.concatenate(shifts(h, 1 << l), axis=0)
            a = jnp.dot(wide, x, preferred_element_type=F32)
            part = U.at[l, chip_rows(chip)]
            part[...] = jax.nn.gelu(a, approximate=True).astype(BF)
            for o in range(1, G):
                rc(part, part, gat_s.at[l, o], gat_r.at[l, chip], chip_dev(peer(o))).start()
            if l == 0:
                wide = expand(wraw[1, chip])
                load_m.wait()
                c_mix.wait_recv()
            for o in range(1, G):
                c = peer(o)
                other = U.at[l, chip_rows(c)]
                rc(other, other, gat_s.at[l, o], gat_r.at[l, c], chip_dev(c)).wait_recv()
            h = mixed(h, wfull[l, chip].reshape(ch, C), U[l]).astype(F32)
        hout[...] = h.astype(BF)
        for c in range(G):
            hop(c).start()
        load_p.wait()

    def hop(c):
        return rc(hout, hall.at[chip], hop_s.at[c], hop_r.at[chip], (1, c * 2 + core, blk))

    def fetch():
        for kind in range(2):
            for o in range(1, G):
                push(kind, o, chip).start()
        c_mix_one.start()
        load_p.wait()
        move = ones(iota((half_ch, ch), 1) == iota((half_ch, ch), 0) + core * half_ch)
        wown[...] = turned(pw_ref[...], move).astype(BF)
        c_own.start()
        c_own.wait_recv()
        wproj[my_e, chip_rows(chip)] = wown[my_e] + wsib[my_e]

    def share4(o, c):
        part = h4.at[chip_rows(c)]
        return rc(part, part, gat_s.at[0, o], gat_r.at[0, c], chip_dev(peer(o)))

    def encode_second():
        load_m.wait()
        for kind, onward in enumerate((c_conv_all, c_mix_all)):
            for o in range(1, G):
                push(kind, o, peer(o)).wait_recv()
            onward.start()
        for o in range(1, G):
            push(2, o, chip).start()
        c_conv_all.wait_recv()
        for l in range(2):
            for c in range(G):
                wconv[l, c] = expand(wraw[l, c])
        for c in range(G):
            rc(hout, hall.at[c], hop_s.at[c], hop_r.at[c], me_sib).wait_recv()
        h = hall[...].reshape(C, T).astype(F32)
        for l in range(2):
            sides = shifts(h, 4 << l)
            for c in range(G):
                x = jnp.concatenate([v[c * ch : (c + 1) * ch] for v in sides], axis=0)
                a = jnp.dot(wconv[l, c], x, preferred_element_type=F32)
                U[l, c * ch : (c + 1) * ch] = jax.nn.gelu(a, approximate=True).astype(BF)
            if l == 0:
                c_mix_all.wait_recv()
                hall[...] = mixed(h, wfull[0].reshape(C, C), U[0]).reshape(G, ch, T)
                h = hall[...].reshape(C, T).astype(F32)
        c_mix_one.wait_recv()
        last = mixed(hall[chip].astype(F32), wfull[1, chip].reshape(ch, C), U[1])
        h4[chip_rows(chip)] = last
        for o in range(1, G):
            share4(o, chip).start()
        for o in range(1, G):
            push(2, o, peer(o)).wait_recv()
        c_wp.start()
        for o in range(1, G):
            share4(o, peer(o)).wait_recv()
        c_wp.wait_recv()
        p = jnp.dot(wproj[...], h4[...], preferred_element_type=F32)
        norm = lax.rsqrt(jnp.sum(p * p, axis=0, keepdims=True) / E + 1e-6)
        D[blk, core] = (p * norm).astype(BF)

    def prepare():
        load_r.wait()
        lanes = E // T
        r32[:, 0:8] = jnp.zeros((lanes, 8, T), F32)
        r32[:, F + 8 : F + 16] = jnp.zeros((lanes, 8, T), F32)

        @pl.loop(0, F // 64)
        def _(i):
            at = pl.multiple_of(i * 64, 64)
            for b in range(lanes):
                piece = rbuf[pl.ds(at, 64), b * T : (b + 1) * T]
                r32[b, pl.ds(at + 8, 64)] = piece.astype(F32)

        @pl.loop(0, (LO + 2 * PAD) // 4)
        def _(i):
            for k in range(2):
                at = i * 4 + k * 2 + 8 - PAD
                to = pl.multiple_of(i * 32 + k * 16, 16)
                for b in range(lanes):
                    two = jnp.concatenate(
                        [r32[b, pl.ds(at + v, SUB, stride=LO), :] for v in range(2)], axis=0
                    )
                    rperm[pl.ds(to, 16), b * T : (b + 1) * T] = two.astype(BF)

        ends = []
        total = jnp.int32(0)
        for k in range(slices):
            total = total + sl_ref[0, k]
            ends.append(total)

        @pl.loop(0, LO // 8)
        def _(i):
            shape = (8, SUB, T)
            lo = lax.broadcasted_iota(jnp.int32, shape, 0) + i * 8
            r = lax.broadcasted_iota(jnp.int32, shape, 1) * LO + lo
            begin = jnp.zeros(shape, jnp.int32)
            end = jnp.full(shape, F, jnp.int32)
            for e in ends:
                begin = jnp.maximum(begin, jnp.where(r >= e, e, 0))
                end = jnp.minimum(end, jnp.where(r < e, e, F))
            t = (lax.broadcasted_iota(jnp.int32, shape, 2) + lo) & (T - 1)
            at = pl.ds(i * 8, 8)
            for k in range(TAPS):
                j = k - MID
                if j == 0:
                    continue
                inside = jnp.where((r + j >= begin) & (r + j < end), taps_ref[k] / taps_ref[MID], 0.0)
                wtab[k, at] = jnp.where((t + j >= 0) & (t + j < T), inside, 0.0)

    def multiply(z, into):
        both = jnp.concatenate([D[z, 0], D[z, 1]], axis=1)
        s = jnp.dot(rperm[...], both, preferred_element_type=F32)
        for i in range(LO + 2 * PAD):
            for n in range(2):
                piece = s[i * SUB : (i + 1) * SUB, n * T : (n + 1) * T]
                into[n, i] = pltpu.roll(piece, (2 * LO + PAD - i) % T, 1)

    def select(z, s):
        for side in range(2):
            best = [None, None]
            for lo in range(side * LO // 2, (side + 1) * LO // 2, GROUP):
                w = [None if k == MID else wtab[k, lo : lo + GROUP] for k in range(TAPS)]
                for n in range(2):
                    win = s[n, lo + PAD - MID : lo + PAD + MID + GROUP]
                    t = [win[k : k + GROUP] for k in range(TAPS)]
                    t = [v if k == MID else w[k] * v for k, v in enumerate(t)]
                    f = (t[0] + t[1]) + (t[2] + t[3]) + (t[4] + t[5] + t[6])
                    f = jnp.max(f, axis=0)
                    best[n] = f if best[n] is None else jnp.maximum(best[n], f)
            for n in range(2):
                acc[(z * 2 + n) * 2 + side] = best[n]

    def run(new, into, old, held):
        if old is not None:
            select(old, held)
        if new is not None:
            multiply(new, into)

    def bit(z, k):
        return D.at[z, core, pl.ds(pl.multiple_of(k * ec, ec), ec)]

    def cross(k):
        ref = bit(blk, k)
        return rc(ref, ref, cross_s.at[k], cross_r.at[k], (1 - phase, across, blk))

    def ring(way, step, k):
        ref = bit(slot((1 - way * 2) * (1 - step)), k)
        sems = ring_s.at[way, step, k], ring_r.at[way, step, k]
        return rc(ref, ref, *sems, (up, down)[way])

    def arrival(way, step, k):
        ref = bit(slot((way * 2 - 1) * step), k)
        sems = ring_s.at[way, step, k], ring_r.at[way, step, k]
        return rc(ref, ref, *sems, (up, down)[way])

    def hand(z):
        ref = D.at[z, core]
        return rc(ref, ref, sib_s.at[8 + z], sib_r.at[8 + z], me_sib)

    def handed(z):
        ref = D.at[z, 1 - core]
        return rc(ref, ref, sib_s.at[8 + z], sib_r.at[8 + z], me_sib)

    def order(i):
        return slot((i + 1) // 2 * (1 - 2 * lax.rem(i, 2)))

    half = CHUNKS // 2
    far = order(Z - 1)

    pl.when(first)(encode_first)
    pl.when(second)(fetch)
    prepare()

    @pl.when(second)
    def _():
        encode_second()
        for k in range(CHUNKS):
            cross(k).start()

    for k in range(CHUNKS):
        @pl.when(first)
        def _():
            cross(k).wait_recv()

        for way in range(2):
            ring(way, 1, k).start()
    hand(blk).start()

    handed(blk).wait_recv()
    run(blk, s1, None, None)

    def relay(step, k):
        for way in range(2):
            arrival(way, step, k).wait_recv()

            @pl.when((step < H - 1) | (k // half == way))
            def _():
                ring(way, step + 1, k).start()

    def hand_both(step):
        for way in range(2):
            hand(slot((way * 2 - 1) * step)).start()

    for k in range(CHUNKS):
        relay(1, k)
    hand_both(1)

    @pl.loop(2, H + 1)
    def _(step):
        @pl.when(step < H)
        def _():
            for k in range(CHUNKS):
                relay(step, k)
            hand_both(step)

        for v in range(2):
            i = 2 * step - 3 + v
            handed(order(i)).wait_recv()
            run(order(i), (s0, s1)[v], order(i - 1), (s1, s0)[v])

            if v == 0:
                @pl.when(step == H)
                def _():
                    for k in range(CHUNKS):
                        arrival(k // half, H, k).wait_recv()
                    hand(far).start()

    handed(far).wait_recv()
    run(far, s0, order(Z - 2), s1)
    run(None, None, far, s0)

    wide = acc.shape[0] * SUB
    flat = jnp.max(acc[...].reshape(wide, T).T, axis=0, keepdims=True)
    flat = flat * (taps_ref[MID] * E ** (-0.5))
    lane = iota((2 * Z, wide), 1)
    apart = jnp.where(lane // (2 * SUB) == iota((2 * Z, wide), 0), flat, 0.0)
    lane = iota((wide, 2 * SUB), 0)
    tile = lane % SUB * 2 + lane // SUB % 2
    pick = (tile == iota((wide, 2 * SUB), 1)).astype(F32)
    out_ref[...] = jnp.dot(
        apart, pick, preferred_element_type=F32, precision=lax.Precision.HIGHEST
    )

    @pl.when(first)
    def _():
        c_conv.wait_send()
        c_mix.wait_send()
        c_q.wait_send()
        for l in range(2):
            for o in range(1, G):
                part = U.at[l, chip_rows(chip)]
                rc(part, part, gat_s.at[l, o], gat_r.at[l, chip], chip_dev(peer(o))).wait_send()
        for c in range(G):
            hop(c).wait_send()

    @pl.when(second)
    def _():
        c_own.wait_send()
        c_wp.wait_send()
        c_conv_all.wait_send()
        c_mix_all.wait_send()
        c_mix_one.wait_send()
        for kind in range(3):
            for o in range(1, G):
                push(kind, o, chip).wait_send()
        for o in range(1, G):
            share4(o, chip).wait_send()
        for k in range(CHUNKS):
            cross(k).wait_send()

    for i in range(Z):
        hand(i).wait_send()
    for k in range(CHUNKS):
        for way in range(2):
            for step in range(1, H):
                ring(way, step, k).wait_send()
        ring(k // half, H, k).wait_send()


def solution(mesh):
    G = mesh.shape["bank"] // 2
    Z = mesh.shape["blk"]

    def per_device(q, cw, mw, pw, taps, rf, sl):
        half_ch, T = q.shape[1:]
        ch = 2 * half_ch
        C = mw.shape[2]
        E = pw.shape[0]
        F = rf.shape[0]
        LO = F // SUB
        dma = pltpu.SemaphoreType.DMA
        vmem = pl.BlockSpec(memory_space=pltpu.VMEM)
        smem = pl.BlockSpec(memory_space=pltpu.SMEM)
        anyw = pl.BlockSpec(memory_space=pl.ANY)
        cw = jnp.transpose(cw, (0, 1, 3, 2))
        pw = jnp.transpose(pw)
        return pl.pallas_call(
            functools.partial(kernel, G, Z),
            out_shape=jax.ShapeDtypeStruct((2 * Z, 2 * SUB), F32),
            in_specs=[anyw, anyw, anyw, anyw, smem, anyw, smem],
            out_specs=vmem,
            scratch_shapes=[
                pltpu.VMEM(q.shape, BF),
                pltpu.VMEM(cw.shape, BF),
                pltpu.VMEM(pw.shape, BF),
                pltpu.VMEM((2, G, 2, half_ch, T), BF),
                pltpu.VMEM((2, G, ch, 3 * ch), BF),
                pltpu.VMEM((2, G, 2, half_ch, C), BF),
                pltpu.VMEM((E, ch), BF),
                pltpu.VMEM((E, ch), BF),
                pltpu.VMEM((E, C), BF),
                pltpu.VMEM((ch, T), BF),
                pltpu.VMEM((ch, T), BF),
                pltpu.VMEM((G, ch, T), BF),
                pltpu.VMEM((C, T), BF),
                pltpu.VMEM((2, C, T), BF),
                pltpu.VMEM((Z, 2, E, T), BF),
                pltpu.VMEM((F, E), BF),
                pltpu.VMEM((E // T, F + 16, T), F32),
                pltpu.VMEM(((LO + 2 * PAD) * SUB, E), BF),
                pltpu.VMEM((TAPS, LO, SUB, T), F32),
                pltpu.VMEM((2, LO + 2 * PAD, SUB, T), F32),
                pltpu.VMEM((2, LO + 2 * PAD, SUB, T), F32),
                pltpu.VMEM((Z * 4, SUB, T), F32),
                dma((5,)),
                dma((8 + Z,)),
                dma((8 + Z,)),
                dma((2, G)),
                dma((2, G)),
                dma((G,)),
                dma((G,)),
                dma((3, G)),
                dma((3, G)),
                dma((2, Z // 2 + 1, CHUNKS)),
                dma((2, Z // 2 + 1, CHUNKS)),
                dma((CHUNKS,)),
                dma((CHUNKS,)),
            ],
            compiler_params=pltpu.CompilerParams(
                collective_id=0,
                has_side_effects=True,
                vmem_limit_bytes=60 * 1024 * 1024,
            ),
        )(q, cw, mw, pw, taps, rf, sl)

    return jax.shard_map(
        per_device,
        mesh=mesh,
        in_specs=(
            P("blk", "bank", None),
            P("phase", None, "bank", None),
            P("phase", "bank", None),
            P(None, "bank"),
            P(),
            P(("phase", "bank", "blk"), None),
            P(("phase", "bank", "blk"), None),
        ),
        out_specs=P(None, ("phase", "bank", "blk")),
        check_vma=False,
    )
```
